256 devices in a mesh: ctx: 64 (over x, z, core), rep: 4 (over y).
Axes of the slice: x: 4, y: 4, z: 8, core: 2. Of those that a mesh axis runs over, the one named last changes fastest.
Arguments:
- queries: bfloat16 [8, 2, 128, 192], P('rep', None, 'ctx'), parts along dimension 0, may hold values from -6 to 6
- key_absorb: bfloat16 [128, 128, 512], P('ctx'), may hold values from -0.5 to 0.5
- latent_cache: bfloat16 [8, 262144, 576], P('rep', 'ctx'), parts along dimension 0, may hold values from -600 to 600
- page_order: int32 [8, 2048], P('rep', 'ctx'), parts along dimension 0, may hold values from 0 to 2047, each once within a row
- lengths: int32 [8], P('rep'), parts along dimension 0, may hold values from 65536 to 262144
- kerple_scale: float32 [128], replicated, may hold values from 0.05 to 2
- kerple_rate: float32 [128], replicated, may hold values from 0.005 to 0.5
- value_up: bfloat16 [128, 512, 128], P('ctx'), may hold values from -0.25 to 0.25
- output_weight: bfloat16 [16384, 7168], P('ctx'), may hold values from -0.125 to 0.125
Outputs:
- attn_out: bfloat16 [8, 2, 7168], P('rep', None, 'ctx'), parts along dimension 0
The draws below stay inside these ranges and needn't reach their ends.
There are 4 independent parts, one for each index of `rep`. The reference program is written for one: setup_inputs(seed, part) draws one part's arguments, and reference() takes and returns one part's arrays. A program takes and returns all parts, laid end to end along the dimension named above; an argument that names none is the same for every part. Nothing has to cross between parts.
All inputs are finite; a program needn't handle non-finite values.
Results may differ from the reference program's by a relative error of at most 0.015.
Values may be sent and summed in bfloat16 or wider, within the bound.
A program may use at most 192 MiB of HBM per device.

```python
import math
import jax
import jax.numpy as jnp
from jax import lax

HEADS = 128
NOPE = 128
ROPE = 64
LAT = 512
VDIM = 128
D = 7168
REQ = 2
QLEN = 2
PAGE = 128
CTXLEN = 262144
PAGES = 2048


def draw_latent_cache(key, part):
    key = jax.random.fold_in(key, 7)
    base_key = jax.random.fold_in(key, 0)
    full_shape = (REQ, CTXLEN, LAT + ROPE)
    baseline = jnp.clip(jax.random.normal(base_key, full_shape, jnp.float32), -6.0, 6.0)
    values = baseline
    return values.astype(jnp.bfloat16)


def strengthened(array, own_key, source, target, blocks, factor):
    owner, partner = [(jnp.arange(array.shape[position]) // (array.shape[position] // blocks)).reshape([-1 if axis == position else 1 for axis in range(array.ndim)]) for position in (source, target)]
    chosen = jax.random.permutation(own_key, blocks)[partner]
    strong = (owner == chosen) | (owner == (partner + blocks // 2) % blocks)
    return jnp.where(strong, factor * array, array)


def steps_of(own_key, shape, shards, low, top_value):
    factor_of = 1.0
    for dim, blocks in shards:
        draws = jax.random.uniform(jax.random.fold_in(jax.random.fold_in(own_key, 6), dim), (blocks,), jnp.float32, low / len(shards), top_value / len(shards))
        factor_of = factor_of * jnp.repeat(jnp.exp(draws), shape[dim] // blocks).reshape((-1,) + (1,) * (len(shape) - 1 - dim))
    return factor_of


def noise(own_key, dims, scale, limit, cuts=(), held_as=jnp.bfloat16):
    values = scale * jax.random.normal(own_key, dims, jnp.float32)
    if cuts:
        values = values * steps_of(own_key, dims, cuts, -0.22, 0.18)
    return jnp.clip(values, -limit, limit).astype(held_as)


def noise_with(rng, dims, width, bound, pieces, heavy, held_as=jnp.bfloat16):
    result = width * jax.random.normal(rng, dims, jnp.float32)
    if pieces:
        result = result * steps_of(rng, dims, pieces, -0.22, 0.18)
    return jnp.clip(strengthened(result, jax.random.fold_in(rng, 3), *heavy), -bound, bound).astype(held_as)


def setup_inputs(seed: int = 0, part: int = 0) -> dict:
    seeds = jax.random.split(jax.random.key(seed), 10)
    part_keys = jax.random.split(jax.random.fold_in(seeds[9], part), 10)
    return {
        "queries": noise(part_keys[0], (REQ, QLEN, HEADS, NOPE + ROPE), 1.0, 6.0, ((2, 64),)),
        "key_absorb": noise(seeds[1], (HEADS, NOPE, LAT), NOPE ** -0.5, 0.5, ((0, 64),)),
        "latent_cache": draw_latent_cache(jax.random.fold_in(jax.random.fold_in(seeds[9], part), 71), part),
        "page_order": jax.vmap(lambda own: jax.random.permutation(own, PAGES))(jax.random.split(part_keys[3], REQ)).reshape((REQ, PAGES)).astype(jnp.int32),
        "lengths": jax.random.randint(part_keys[4], (REQ,), CTXLEN // 4, CTXLEN + 1).astype(jnp.int32),
        "kerple_scale": jnp.clip(jnp.exp(jax.random.uniform(seeds[5], (HEADS,), jnp.float32, math.log(0.05), math.log(2.0))), 0.05, 2.0),
        "kerple_rate": jnp.clip(jnp.exp(jax.random.uniform(seeds[6], (HEADS,), jnp.float32, math.log(0.005), math.log(0.5))), 0.005, 0.5),
        "value_up": noise(seeds[7], (HEADS, LAT, VDIM), LAT ** -0.5, 0.25, ((0, 64),)),
        "output_weight": noise_with(seeds[8], (HEADS * VDIM, D), (HEADS * VDIM) ** -0.5, 0.125, ((0, 64),), (0, 1, 64, 4.0)),
    }


masked_score = -1.0e30


def reference(queries, key_absorb, latent_cache, page_order, lengths, kerple_scale, kerple_rate, value_up, output_weight):
    latent_query = jnp.einsum('bqhn,hnc->bqhc', queries[..., :NOPE].astype(jnp.float32), key_absorb.astype(jnp.float32)).astype(jnp.bfloat16)
    full_query = jnp.concatenate([latent_query, queries[..., NOPE:]], axis=-1)
    offsets = jnp.arange(PAGE, dtype=jnp.int32)
    key_pos = (page_order[:, :, None] * PAGE + offsets[None, None, :]).reshape(REQ, CTXLEN).astype(jnp.int32)
    query_pos = (lengths[:, None] - QLEN + jnp.arange(QLEN, dtype=jnp.int32)[None, :]).astype(jnp.int32)
    softmax_scale = (NOPE + ROPE) ** -0.5

    def per_request(items):
        request_query, request_cache, request_keys, request_pos = items
        distance = request_pos[:, None] - request_keys[None, :]
        visible = distance >= 0
        spread = jnp.maximum(distance, 0).astype(jnp.float32)
        flat_query = request_query.reshape(QLEN * HEADS, LAT + ROPE)
        scores = jnp.dot(flat_query, request_cache.T, preferred_element_type=jnp.float32).reshape(QLEN, HEADS, CTXLEN)
        log_bias = kerple_scale[None, :, None] * jnp.log1p(kerple_rate[None, :, None] * spread[:, None, :])
        scores = jnp.where(visible[:, None, :], scores * softmax_scale - log_bias, masked_score)
        row_max = jnp.max(scores, axis=-1, keepdims=True)
        weights = jnp.where(visible[:, None, :], jnp.exp(scores - row_max), 0.0)
        row_total = jnp.sum(weights, axis=-1)
        summed = jnp.dot(weights.reshape(QLEN * HEADS, CTXLEN).astype(jnp.bfloat16), request_cache[:, :LAT], preferred_element_type=jnp.float32)
        return (summed.reshape(QLEN, HEADS, LAT) / row_total[..., None]).astype(jnp.bfloat16)

    attn_latent = lax.map(per_request, (full_query, latent_cache, key_pos, query_pos))
    up_values = jnp.einsum('bqhc,hcv->bqhv', attn_latent.astype(jnp.float32), value_up.astype(jnp.float32)).astype(jnp.bfloat16)
    flat_values = up_values.reshape(REQ * QLEN, HEADS * VDIM)
    return jnp.dot(flat_values, output_weight, preferred_element_type=jnp.float32).reshape(REQ, QLEN, D).astype(jnp.bfloat16)
```

```python
import functools
import math

import jax
import jax.numpy as jnp
from jax import lax
from jax.experimental import pallas as pl
from jax.experimental.pallas import tpu as pltpu
from jax.sharding import PartitionSpec as P

MESH = pl.DeviceIdType.MESH
F32 = jnp.float32
BF16 = jnp.bfloat16

NX, NZ, NC = 4, 8, 2
NXC = NX * NC
LAT, ROPE, NOPE, VDIM = 512, 64, 128, 128
WIDE = 640
SLOTS = 4096
PAGE = 128
D = 7168
DOUT = D // (NX * NZ * NC)
ROWS = 256
CHUNK = 1024
SIGMA = (NOPE + ROPE) ** -0.5
KAPPA = SIGMA * math.log2(math.e)
FLOOR = -1.0e30


def split3(v):
    hi = v.astype(BF16).astype(F32)
    rest = v - hi
    mid = rest.astype(BF16).astype(F32)
    return hi, mid, rest - mid


def pack_stats(c, l):
    lane = lax.broadcasted_iota(jnp.int32, c.shape, c.ndim - 1)
    out = jnp.zeros_like(c)
    for i, part in enumerate(split3(c) + split3(l)):
        out = jnp.where(lane == i, part, out)
    return out


def unpack_stats(st):
    lane = lax.broadcasted_iota(jnp.int32, st.shape, st.ndim - 1)
    c = jnp.sum(jnp.where(lane < 3, st, 0.0), axis=-1, keepdims=True)
    l = jnp.sum(jnp.where((lane >= 3) & (lane < 6), st, 0.0), axis=-1, keepdims=True)
    return c, l


def merge(parts):
    stats = [unpack_stats(p[..., LAT:]) for p in parts]
    c = stats[0][0]
    for ci, _ in stats[1:]:
        c = jnp.maximum(c, ci)
    total, l = None, None
    for p, (ci, li) in zip(parts, stats):
        f = jnp.exp2(KAPPA * (ci - c))
        term, lt = p[..., :LAT] * f, li * f
        total = term if total is None else total + term
        l = lt if l is None else l + lt
    return total, c, l


def kernel(
    q_hbm, ka_hbm, kt_hbm, page_ref, len_ref, scale_ref, rate_ref, vu_hbm, w_hbm,
    out_ref,
    q_s, x_s, ka_s, kt_s, vu_s, w_s,
    ag1, qall, s_buf, acc, rate_b, scale_b,
    rs1_send, rs1_recv, held, rs2_send, rs2_recv, o1_send, o1_recv, o2_send, o2_recv,
    local_sem, ag1_ss, ag1_rs, ag2_ss, ag2_rs, rs1_ss, rs1_rs, rs2_ss, rs2_rs,
    o1_ss, o1_rs, o2_ss, o2_rs,
):
    ctx = lax.axis_index("ctx")
    rep = lax.axis_index("rep")
    x, z, c = ctx // (NZ * NC), (ctx // NC) % NZ, ctx % NC
    xc = x * NC + c

    def z_peer(zz):
        return ((x * NZ + zz) * NC + c, rep)

    def xc_peer(o):
        return (((o // NC) * NZ + z) * NC + o % NC, rep)

    barrier = pltpu.get_barrier_semaphore()
    for k in range(1, 8):
        pl.semaphore_signal(barrier, inc=1, device_id=z_peer((z + k) % NZ), device_id_type=MESH)
        pl.semaphore_signal(barrier, inc=1, device_id=xc_peer((xc + k) % NXC), device_id_type=MESH)

    loads = [
        pltpu.make_async_copy(q_hbm, q_s, local_sem.at[0]),
        pltpu.make_async_copy(ka_hbm, ka_s, local_sem.at[1]),
        pltpu.make_async_copy(kt_hbm.at[0], kt_s.at[0, pl.ds(0, LAT + ROPE)], local_sem.at[2]),
        pltpu.make_async_copy(kt_hbm.at[1], kt_s.at[1, pl.ds(0, LAT + ROPE)], local_sem.at[3]),
        pltpu.make_async_copy(vu_hbm, vu_s, local_sem.at[4]),
        pltpu.make_async_copy(w_hbm, w_s, local_sem.at[5]),
    ]
    for load in loads:
        load.start()

    loads[0].wait()
    for r in range(2):
        for q in range(2):
            x_s[pl.ds(4 * r + 2 * q, 2), :] = q_s[r, q].astype(F32)
    loads[1].wait()
    xq = x_s[...]
    nope = xq[:, :NOPE].astype(BF16)
    lat0 = jnp.dot(nope, ka_s[0], preferred_element_type=F32)
    lat1 = jnp.dot(nope, ka_s[1], preferred_element_type=F32)
    row8 = lax.broadcasted_iota(jnp.int32, (8, LAT), 0)
    ag1[z, :, pl.ds(0, LAT)] = jnp.where(row8 % 2 == 0, lat0, lat1).astype(BF16)
    ag1[z, :, pl.ds(LAT, 128)] = jnp.zeros((8, 128), BF16)
    ag1[z, :, pl.ds(LAT, ROPE)] = xq[:, NOPE:].astype(BF16)

    pl.semaphore_wait(barrier, 14)

    def ag1_copy(k, slot):
        return pltpu.make_async_remote_copy(
            src_ref=ag1.at[slot], dst_ref=ag1.at[slot],
            send_sem=ag1_ss.at[k], recv_sem=ag1_rs.at[slot],
            device_id=z_peer((z + k) % NZ), device_id_type=MESH)

    for k in range(1, 8):
        ag1_copy(k, z).start()

    for r in range(2):
        kt_s[r, pl.ds(LAT + ROPE, 64), :] = jnp.zeros((64, SLOTS), BF16)
    row = lax.broadcasted_iota(jnp.int32, (ROWS, 128), 0)
    lane = lax.broadcasted_iota(jnp.int32, (ROWS, 128), 1)
    head = (row // 64) * 32 + ((row // 4) % 8) * 4 + ((row // 32) % 2) * 2 + row % 2
    hot = lane == head
    rate_col = jnp.sum(jnp.where(hot, rate_ref[...], 0.0), axis=-1, keepdims=True)
    scale_col = jnp.sum(jnp.where(hot, scale_ref[...], 0.0), axis=-1, keepdims=True)
    rate_b[...] = jnp.broadcast_to(rate_col, (ROWS, 128))
    scale_b[...] = jnp.broadcast_to(scale_col * (1.0 / SIGMA), (ROWS, 128))
    o1_send[...] = jnp.zeros_like(o1_send)

    for k in range(1, 8):
        ag1_copy(k, (z + k) % NZ).wait_recv()

    blocks = ag1[...].astype(F32).reshape(4, 2, 8, WIDE)
    even, odd = blocks[:, 0], blocks[:, 1]
    sub = lax.broadcasted_iota(jnp.int32, (4, 8, WIDE), 1)
    first = jnp.where(sub < 4, even, pltpu.roll(odd, 4, 1))
    second = jnp.where(sub < 4, pltpu.roll(even, 4, 1), odd)
    qall[0, xc] = first.reshape(32, WIDE).astype(BF16)
    qall[1, xc] = second.reshape(32, WIDE).astype(BF16)

    def ag2_copy(r, k, slot):
        return pltpu.make_async_remote_copy(
            src_ref=qall.at[r, slot], dst_ref=qall.at[r, slot],
            send_sem=ag2_ss.at[r, k], recv_sem=ag2_rs.at[r, slot],
            device_id=xc_peer((xc + k) % NXC), device_id_type=MESH)

    for r in range(2):
        for k in range(1, 8):
            ag2_copy(r, k, xc).start()

    sub8 = lax.broadcasted_iota(jnp.int32, (8, 128), 0)
    lane8 = lax.broadcasted_iota(jnp.int32, (8, 128), 1)
    offset = ((sub8 // 2) % 2 - lane8).astype(F32)

    def attention(r):
        full_query = qall[r].reshape(ROWS, WIDE)
        rate = rate_b[...].reshape(32, 8, 128)
        scale = scale_b[...].reshape(32, 8, 128)
        base = len_ref[r] - 2

        def scores(i, peak):
            cols = pl.ds(pl.multiple_of(i * CHUNK, CHUNK), CHUNK)
            s = jnp.dot(full_query, kt_s[r, :, cols], preferred_element_type=F32)
            for p in range(CHUNK // PAGE):
                page = page_ref[r, i * (CHUNK // PAGE) + p]
                dist = (base - page * PAGE).astype(F32) + offset
                dist = jnp.where(dist >= 0.0, dist, jnp.inf)
                bias = scale * jnp.log(1.0 + rate * dist[None])
                u = s[:, p * PAGE:(p + 1) * PAGE].reshape(32, 8, 128) - bias
                s_buf[:, pl.ds(pl.multiple_of(i * CHUNK + p * PAGE, PAGE), PAGE)] = u.reshape(ROWS, 128)
                peak = jnp.maximum(peak, u)
            return peak

        peak = lax.fori_loop(0, SLOTS // CHUNK, scores, jnp.full((32, 8, 128), FLOOR, F32))
        shift = jnp.max(peak, axis=-1, keepdims=True)
        acc[...] = jnp.zeros_like(acc)

        def sums(i, total):
            weights = []
            for p in range(CHUNK // PAGE):
                u = s_buf[:, pl.ds(pl.multiple_of(i * CHUNK + p * PAGE, PAGE), PAGE)]
                w = jnp.exp2(KAPPA * (u.reshape(32, 8, 128) - shift))
                total = total + w
                weights.append(w.reshape(ROWS, 128).astype(BF16))
            cols = pl.ds(pl.multiple_of(i * CHUNK, CHUNK), CHUNK)
            acc[...] += lax.dot_general(
                jnp.concatenate(weights, axis=1), kt_s[r, pl.ds(0, LAT), cols],
                (((1,), (1,)), ((), ())), preferred_element_type=F32)
            return total

        total = lax.fori_loop(0, SLOTS // CHUNK, sums, jnp.zeros((32, 8, 128), F32))
        total = jnp.sum(total, axis=-1, keepdims=True)
        return shift, total

    def rs1_copy(r, k, src, dst):
        return pltpu.make_async_remote_copy(
            src_ref=rs1_send.at[r, src], dst_ref=rs1_recv.at[r, dst],
            send_sem=rs1_ss.at[r, k], recv_sem=rs1_rs.at[r, dst],
            device_id=xc_peer((xc + k) % NXC), device_id_type=MESH)

    def send_partials(r, shift, total):
        stats = pack_stats(
            jnp.broadcast_to(shift, (32, 8, 128)), jnp.broadcast_to(total, (32, 8, 128)))
        rs1_send[r, :, :, pl.ds(0, LAT)] = acc[...].astype(BF16).reshape(NXC, 32, LAT)
        rs1_send[r, :, :, pl.ds(LAT, 128)] = stats.reshape(ROWS, 128).astype(BF16).reshape(NXC, 32, 128)
        for k in range(1, 8):
            rs1_copy(r, k, (xc + k) % NXC, xc).start()
        rs1_recv[r, xc] = rs1_send[r, xc]

    def merge_first(r):
        for k in range(1, 8):
            rs1_copy(r, k, xc, (xc + k) % NXC).wait_recv()
        total, shift, l = merge([rs1_recv[r, o].astype(F32).reshape(4, 8, WIDE) for o in range(NXC)])
        stats = pack_stats(jnp.broadcast_to(shift, (4, 8, 128)), jnp.broadcast_to(l, (4, 8, 128)))
        return total, stats

    loads[2].wait()
    for k in range(1, 8):
        ag2_copy(0, k, (xc + k) % NXC).wait_recv()
    send_partials(0, *attention(0))
    loads[3].wait()
    for k in range(1, 8):
        ag2_copy(1, k, (xc + k) % NXC).wait_recv()
    send_partials(1, *attention(1))

    sum0, st0 = merge_first(0)
    sum1, st1 = merge_first(1)

    for r0, r1, width, at in ((sum0, sum1, LAT, 0), (st0, st1, 128, LAT)):
        sub = lax.broadcasted_iota(jnp.int32, (4, 8, width), 1)
        even = jnp.where(sub < 4, r0, pltpu.roll(r1, 4, 1))
        odd = jnp.where(sub < 4, pltpu.roll(r0, 4, 1), r1)
        for g in range(4):
            rs2_send[2 * g, :, pl.ds(at, width)] = even[g].astype(BF16)
            rs2_send[2 * g + 1, :, pl.ds(at, width)] = odd[g].astype(BF16)

    def rs2_copy(k, src, dst):
        return pltpu.make_async_remote_copy(
            src_ref=rs2_send.at[src], dst_ref=rs2_recv.at[dst],
            send_sem=rs2_ss.at[k], recv_sem=rs2_rs.at[dst],
            device_id=z_peer((z + k) % NZ), device_id_type=MESH)

    for k in range(1, 8):
        rs2_copy(k, (z + k) % NZ, z).start()
    rs2_recv[z] = rs2_send[z]
    loads[4].wait()
    loads[5].wait()
    for k in range(1, 8):
        rs2_copy(k, z, (z + k) % NZ).wait_recv()
    total, _, l = merge([rs2_recv[o].astype(F32).reshape(1, 8, WIDE) for o in range(NZ)])
    latent = (total / l).reshape(8, LAT).astype(BF16)

    up0 = jnp.dot(latent, vu_s[0], preferred_element_type=F32)
    up1 = jnp.dot(latent, vu_s[1], preferred_element_type=F32)
    values = jnp.concatenate([up0, pltpu.roll(up1, 7, 0)], axis=1).astype(BF16)
    share = jnp.dot(values, w_s[...], preferred_element_type=F32)

    even_row = lax.broadcasted_iota(jnp.int32, (8, DOUT), 0) % 2 == 0
    for o in range(NXC):
        for g in range(4):
            j = ((o // NC) * NZ + 2 * g) * NC + o % NC
            a = share[:, j * DOUT:(j + 1) * DOUT]
            b = share[:, (j + NC) * DOUT:(j + NC + 1) * DOUT]
            o1_send[o, g, :, pl.ds(0, DOUT)] = jnp.where(even_row, a, pltpu.roll(b, 1, 0)).astype(BF16)

    def o1_copy(k, src, dst):
        return pltpu.make_async_remote_copy(
            src_ref=o1_send.at[src], dst_ref=o1_recv.at[dst],
            send_sem=o1_ss.at[k], recv_sem=o1_rs.at[dst],
            device_id=xc_peer((xc + k) % NXC), device_id_type=MESH)

    for k in range(1, 8):
        o1_copy(k, (xc + k) % NXC, xc).start()
    o1_recv[xc] = o1_send[xc]
    for k in range(1, 8):
        o1_copy(k, xc, (xc + k) % NXC).wait_recv()
    part = o1_recv[0].astype(F32)
    for o in range(1, NXC):
        part = part + o1_recv[o].astype(F32)
    o2_send[...] = part

    def o2_copy(k, src, dst):
        return pltpu.make_async_remote_copy(
            src_ref=o2_send.at[src], dst_ref=o2_recv.at[dst],
            send_sem=o2_ss.at[k], recv_sem=o2_rs.at[dst],
            device_id=z_peer((z + k) % NZ), device_id_type=MESH)

    for k in range(1, 8):
        o2_copy(k, ((z + k) % NZ) // 2, z).start()
    o2_recv[z] = o2_send[z // 2]
    for k in range(1, 8):
        o2_copy(k, 0, (z + k) % NZ).wait_recv()
    final = o2_recv[0]
    for o in range(1, NZ):
        final = final + o2_recv[o]
    final = jnp.where(z % 2 == 0, final, pltpu.roll(final, 7, 0))
    for r in range(2):
        for q in range(2):
            at = 4 * r + 2 * q
            out_ref[r, pl.ds(q, 1), :] = final[at:at + 1, :DOUT].astype(BF16)

    for k in range(1, 8):
        ag1_copy(k, z).wait_send()
        for r in range(2):
            ag2_copy(r, k, xc).wait_send()
            rs1_copy(r, k, xc, xc).wait_send()
        rs2_copy(k, z, z).wait_send()
        o1_copy(k, xc, xc).wait_send()
        o2_copy(k, 0, z).wait_send()


def per_device(queries, key_absorb, latent_cache, page_order, lengths, kerple_scale, kerple_rate,
               value_up, output_weight):
    any_spec = pl.BlockSpec(memory_space=pl.ANY)
    smem = pl.BlockSpec(memory_space=pltpu.SMEM)
    vmem = pl.BlockSpec(memory_space=pltpu.VMEM)
    dma = pltpu.SemaphoreType.DMA
    return pl.pallas_call(
        kernel,
        out_shape=jax.ShapeDtypeStruct((2, 2, DOUT), BF16),
        in_specs=[any_spec, any_spec, any_spec, smem, smem, vmem, vmem, any_spec, any_spec],
        out_specs=vmem,
        scratch_shapes=[
            pltpu.VMEM((2, 2, 2, NOPE + ROPE), BF16),
            pltpu.VMEM((8, NOPE + ROPE), F32),
            pltpu.VMEM((2, NOPE, LAT), BF16),
            pltpu.VMEM((2, WIDE, SLOTS), BF16),
            pltpu.VMEM((2, LAT, VDIM), BF16),
            pltpu.VMEM((2 * VDIM, D), BF16),
            pltpu.VMEM((NZ, 8, WIDE), BF16),
            pltpu.VMEM((2, NXC, 32, WIDE), BF16),
            pltpu.VMEM((ROWS, SLOTS), F32),
            pltpu.VMEM((ROWS, LAT), F32),
            pltpu.VMEM((ROWS, 128), F32),
            pltpu.VMEM((ROWS, 128), F32),
            pltpu.VMEM((2, NXC, 32, WIDE), BF16),
            pltpu.VMEM((2, NXC, 32, WIDE), BF16),
            pltpu.VMEM((4, 8, WIDE), F32),
            pltpu.VMEM((NZ, 8, WIDE), BF16),
            pltpu.VMEM((NZ, 8, WIDE), BF16),
            pltpu.VMEM((NXC, 4, 8, 128), BF16),
            pltpu.VMEM((NXC, 4, 8, 128), BF16),
            pltpu.VMEM((4, 8, 128), F32),
            pltpu.VMEM((NZ, 8, 128), F32),
            dma((6,)),
            dma((8,)), dma((8,)),
            dma((2, 8)), dma((2, 8)),
            dma((2, 8)), dma((2, 8)),
            dma((8,)), dma((8,)),
            dma((8,)), dma((8,)),
            dma((8,)), dma((8,)),
        ],
        compiler_params=pltpu.CompilerParams(
            collective_id=0, has_side_effects=True, vmem_limit_bytes=56 * 1024 * 1024),
    )(
        queries, key_absorb, jnp.swapaxes(latent_cache, 1, 2), page_order, lengths,
        kerple_scale.reshape(1, 128), kerple_rate.reshape(1, 128), value_up, output_weight,
    )


def solution(mesh):
    in_specs = (
        P("rep", None, "ctx", None),
        P("ctx", None, None),
        P("rep", "ctx", None),
        P("rep", "ctx"),
        P("rep"),
        P(),
        P(),
        P("ctx", None, None),
        P("ctx", None),
    )
    out_specs = P("rep", None, "ctx")
    return jax.shard_map(
        per_device, mesh=mesh, in_specs=in_specs, out_specs=out_specs, check_vma=False
    )
```

```python
import functools
import math

import jax
import jax.numpy as jnp
from jax import lax
from jax.experimental import pallas as pl
from jax.experimental.pallas import tpu as pltpu
from jax.sharding import PartitionSpec as P

MESH = pl.DeviceIdType.MESH
F32 = jnp.float32
BF16 = jnp.bfloat16

NX, NZ, NC = 4, 8, 2
LAT, ROPE, NOPE, VDIM = 512, 64, 128, 128
WIDE = 640
SLOTS = 4096
PAGE = 128
D = 7168
DOUT = D // (NX * NZ * NC)
ROWS = 256
HALF = ROWS // 2
NCHIP = NX * NZ
CHUNK = 1024
SIGMA = (NOPE + ROPE) ** -0.5
KAPPA = SIGMA * math.log2(math.e)
FLOOR = -1.0e30


AWAY = sorted(
    ((dx, dz) for dx in range(NX) for dz in range(NZ) if dx or dz),
    key=lambda d: -min(d[0], NX - d[0]) - min(d[1], NZ - d[1]))


def split3(v):
    hi = v.astype(BF16).astype(F32)
    rest = v - hi
    mid = rest.astype(BF16).astype(F32)
    return hi, mid, rest - mid


def pack_stats(c, l):
    lane = lax.broadcasted_iota(jnp.int32, c.shape, c.ndim - 1)
    out = jnp.zeros_like(c)
    for i, part in enumerate(split3(c) + split3(l)):
        out = jnp.where(lane == i, part, out)
    return out


def unpack_stats(st):
    lane = lax.broadcasted_iota(jnp.int32, st.shape, st.ndim - 1)
    c = jnp.sum(jnp.where(lane < 3, st, 0.0), axis=-1, keepdims=True)
    l = jnp.sum(jnp.where((lane >= 3) & (lane < 6), st, 0.0), axis=-1, keepdims=True)
    return c, l


def kernel(
    q_hbm, ka_hbm, kt_hbm, page_hbm, len_hbm, scale_hbm, rate_hbm, vu_hbm, w_hbm,
    out_ref,
    q_s, x_s, ka_s, kt_s, page_s, len_s, scale_s, rate_s, vu_s, w_s,
    qin, qf, qall, s_buf, acc, rate_b, scale_b,
    pair_send, pair_recv, rs_f, rs_send, rs_recv, lat_s, o_pair, o_pair_recv, o_send, o_recv,
    local_sem, ag_ss, ag_rs, relay_ss, relay_rs, pair_ss, pair_rs, rs_ss, rs_rs,
    op_ss, op_rs, o_ss, o_rs,
):
    ctx = lax.axis_index("ctx")
    rep = lax.axis_index("rep")
    chip, c = ctx // NC, ctx % NC
    x, z = chip // NZ, chip % NZ
    sibling = (chip * NC + 1 - c, rep)

    def away_chip(d):
        return ((x + d[0]) % NX) * NZ + (z + d[1]) % NZ

    def away(d):
        return (away_chip(d) * NC + c, rep)

    barrier = pltpu.get_barrier_semaphore()
    for d in AWAY:
        pl.semaphore_signal(barrier, inc=1, device_id=away(d), device_id_type=MESH)
    pl.semaphore_signal(barrier, inc=1, device_id=sibling, device_id_type=MESH)

    loads = {
        name: pltpu.make_async_copy(src, dst, local_sem.at[i])
        for i, (name, src, dst) in enumerate((
            ("q", q_hbm, q_s),
            ("ka", ka_hbm, ka_s),
            ("scale", scale_hbm, scale_s),
            ("rate", rate_hbm, rate_s),
            ("page", page_hbm, page_s),
            ("len", len_hbm, len_s),
            ("k0", kt_hbm.at[0], kt_s.at[0, pl.ds(0, LAT + ROPE)]),
            ("k1", kt_hbm.at[1], kt_s.at[1, pl.ds(0, LAT + ROPE)]),
            ("vu", vu_hbm, vu_s),
            ("w", w_hbm, w_s),
        ))
    }
    for load in loads.values():
        load.start()

    loads["q"].wait()
    for r in range(2):
        for q in range(2):
            for hh in range(2):
                x_s[pl.ds(4 * r + 2 * hh + q, 1), :] = q_s[r, q, pl.ds(hh, 1), :].astype(F32)
    loads["ka"].wait()
    xq = x_s[...]
    nope = xq[:, :NOPE].astype(BF16)
    lat0 = jnp.dot(nope, ka_s[0], preferred_element_type=F32)
    lat1 = jnp.dot(nope, ka_s[1], preferred_element_type=F32)
    row8 = lax.broadcasted_iota(jnp.int32, (8, LAT), 0)
    lat = jnp.where((row8 // 2) % 2 == 0, lat0, lat1)
    for r in range(2):
        qin[r, chip, :, pl.ds(0, LAT)] = lat[4 * r:4 * r + 4].astype(BF16)
        qin[r, chip, :, pl.ds(LAT, 128)] = jnp.zeros((4, 128), BF16)
        qin[r, chip, :, pl.ds(LAT, ROPE)] = xq[4 * r:4 * r + 4, NOPE:].astype(BF16)

    pl.semaphore_wait(barrier, len(AWAY) + 1)

    def ag_copy(r, d):
        return pltpu.make_async_remote_copy(
            src_ref=qin.at[r, chip], dst_ref=qin.at[r, chip],
            send_sem=ag_ss.at[r], recv_sem=ag_rs.at[r],
            device_id=away(d), device_id_type=MESH)

    def ag_all(r):
        return pltpu.make_async_remote_copy(
            src_ref=qin.at[r, pl.ds(0, NCHIP - 1)], dst_ref=qin.at[r, pl.ds(0, NCHIP - 1)],
            send_sem=ag_ss.at[r], recv_sem=ag_rs.at[r],
            device_id=sibling, device_id_type=MESH)

    for r in range(2):
        for d in AWAY:
            ag_copy(r, d).start()

    for r in range(2):
        kt_s[r, pl.ds(LAT + ROPE, 64), :] = jnp.zeros((64, SLOTS), BF16)
    o_pair[...] = jnp.zeros_like(o_pair)
    row = lax.broadcasted_iota(jnp.int32, (ROWS, 128), 0)
    lane = lax.broadcasted_iota(jnp.int32, (ROWS, 128), 1)
    head = ((row // 4) % 32) * 4 + (row // 128) * 2 + (row // 2) % 2
    hot = lane == head
    loads["scale"].wait()
    loads["rate"].wait()
    rate_col = jnp.sum(jnp.where(hot, rate_s[...], 0.0), axis=-1, keepdims=True)
    scale_col = jnp.sum(jnp.where(hot, scale_s[...], 0.0), axis=-1, keepdims=True)
    rate_b[...] = jnp.broadcast_to(rate_col, (ROWS, 128))
    scale_b[...] = jnp.broadcast_to(scale_col * (1.0 / SIGMA), (ROWS, 128))
    loads["page"].wait()
    loads["len"].wait()

    def relay_copy(r, half):
        return pltpu.make_async_remote_copy(
            src_ref=qall.at[r, half], dst_ref=qall.at[r, half],
            send_sem=relay_ss.at[r], recv_sem=relay_rs.at[r],
            device_id=sibling, device_id_type=MESH)

    def relay(r):
        ag_all(r).wait_recv()
        for i in range(NCHIP // 2):
            qf[pl.ds(8 * i, 4), :] = qin[r, 2 * i].astype(F32)
            qf[pl.ds(8 * i + 4, 4), :] = qin[r, 2 * i + 1].astype(F32)
        qall[r, c] = qf[...].astype(BF16)
        relay_copy(r, c).start()

    sub8 = lax.broadcasted_iota(jnp.int32, (8, 128), 0)
    lane8 = lax.broadcasted_iota(jnp.int32, (8, 128), 1)
    offset = (sub8 % 2 - lane8).astype(F32)

    def scores(r, first, last, peak):
        full_query = qall[r].reshape(ROWS, WIDE)
        rate = rate_b[...].reshape(32, 8, 128)
        scale = scale_b[...].reshape(32, 8, 128)
        base = len_s[r] - 2

        def step(i, peak):
            cols = pl.ds(pl.multiple_of(i * CHUNK, CHUNK), CHUNK)
            s = jnp.dot(full_query, kt_s[r, :, cols], preferred_element_type=F32)
            for p in range(CHUNK // PAGE):
                page = page_s[r, i * (CHUNK // PAGE) + p]
                dist = (base - page * PAGE).astype(F32) + offset
                dist = jnp.where(dist >= 0.0, dist, jnp.inf)
                bias = scale * jnp.log(1.0 + rate * dist[None])
                u = s[:, p * PAGE:(p + 1) * PAGE].reshape(32, 8, 128) - bias
                s_buf[:, pl.ds(pl.multiple_of(i * CHUNK + p * PAGE, PAGE), PAGE)] = u.reshape(ROWS, 128)
                peak = jnp.maximum(peak, u)
            return peak

        return lax.fori_loop(first, last, step, peak)

    def sums(r, shift):
        acc[...] = jnp.zeros_like(acc)

        def step(i, total):
            weights = []
            for p in range(CHUNK // PAGE):
                u = s_buf[:, pl.ds(pl.multiple_of(i * CHUNK + p * PAGE, PAGE), PAGE)]
                w = jnp.exp2(KAPPA * (u.reshape(32, 8, 128) - shift))
                total = total + w
                weights.append(w.reshape(ROWS, 128).astype(BF16))
            cols = pl.ds(pl.multiple_of(i * CHUNK, CHUNK), CHUNK)
            acc[...] += lax.dot_general(
                jnp.concatenate(weights, axis=1), kt_s[r, pl.ds(0, LAT), cols],
                (((1,), (1,)), ((), ())), preferred_element_type=F32)
            return total

        total = lax.fori_loop(0, SLOTS // CHUNK, step, jnp.zeros((32, 8, 128), F32))
        return jnp.sum(total, axis=-1, keepdims=True)

    def pair_copy(r):
        return pltpu.make_async_remote_copy(
            src_ref=pair_send.at[r], dst_ref=pair_recv.at[r],
            send_sem=pair_ss.at[r], recv_sem=pair_rs.at[r],
            device_id=sibling, device_id_type=MESH)

    def rows_of(core):
        return pl.ds(pl.multiple_of(core * HALF, HALF), HALF)

    def send_pair(r, shift, total):
        stats = pack_stats(
            jnp.broadcast_to(shift, (32, 8, 128)), jnp.broadcast_to(total, (32, 8, 128)))
        stats = stats.reshape(2, HALF, 128)
        pair_send[r, :, pl.ds(0, LAT)] = acc[rows_of(1 - c), :].astype(BF16)
        pair_send[r, :, pl.ds(LAT, 128)] = jnp.where(c == 0, stats[1], stats[0]).astype(BF16)
        pair_copy(r).start()
        rs_f[:, pl.ds(0, LAT)] = acc[rows_of(c), :]
        rs_f[:, pl.ds(LAT, 128)] = jnp.where(c == 0, stats[0], stats[1])

    def rs_copy(r, d):
        return pltpu.make_async_remote_copy(
            src_ref=rs_send.at[r, away_chip(d)], dst_ref=rs_recv.at[r, chip],
            send_sem=rs_ss.at[r], recv_sem=rs_rs.at[r],
            device_id=away(d), device_id_type=MESH)

    def rs_all(r):
        return pltpu.make_async_remote_copy(
            src_ref=rs_send.at[r, pl.ds(0, NCHIP - 1)], dst_ref=rs_recv.at[r, pl.ds(0, NCHIP - 1)],
            send_sem=rs_ss.at[r], recv_sem=rs_rs.at[r],
            device_id=sibling, device_id_type=MESH)

    def send_rows(r):
        pair_copy(r).wait_recv()
        mine = rs_f[...].reshape(16, 8, WIDE)
        theirs = pair_recv[r].astype(F32).reshape(16, 8, WIDE)
        (c0, l0), (c1, l1) = unpack_stats(mine[..., LAT:]), unpack_stats(theirs[..., LAT:])
        shift = jnp.maximum(c0, c1)
        f0, f1 = jnp.exp2(KAPPA * (c0 - shift)), jnp.exp2(KAPPA * (c1 - shift))
        both = mine[..., :LAT] * f0 + theirs[..., :LAT] * f1
        stats = pack_stats(
            jnp.broadcast_to(shift, (16, 8, 128)), jnp.broadcast_to(l0 * f0 + l1 * f1, (16, 8, 128)))
        for i in range(NCHIP // 2):
            for h in range(2):
                rs_send[r, 2 * i + h, :, pl.ds(0, LAT)] = both[i, 4 * h:4 * h + 4].astype(BF16)
                rs_send[r, 2 * i + h, :, pl.ds(LAT, 128)] = stats[i, 4 * h:4 * h + 4].astype(BF16)
        for d in AWAY:
            rs_copy(r, d).start()
        rs_recv[r, chip] = rs_send[r, chip]

    def finish_rows(r):
        rs_all(r).wait_recv()
        parts = rs_recv[r].astype(F32)
        ci, li = unpack_stats(parts[..., LAT:])
        f = jnp.exp2(KAPPA * (ci - jnp.max(ci, axis=0, keepdims=True)))
        total = jnp.sum(parts[..., :LAT] * f, axis=0)
        lat_s[pl.ds(4 * r, 4), :] = total / jnp.sum(li * f, axis=0)

    def start_peak():
        return jnp.full((32, 8, 128), FLOOR, F32)

    n = SLOTS // CHUNK
    relay(0)
    loads["k0"].wait()
    relay_copy(0, 1 - c).wait_recv()
    shift = jnp.max(scores(0, 0, n, start_peak()), axis=-1, keepdims=True)
    relay(1)
    send_pair(0, shift, sums(0, shift))
    loads["k1"].wait()
    relay_copy(1, 1 - c).wait_recv()
    peak = scores(1, 0, n // 2, start_peak())
    send_rows(0)
    shift = jnp.max(scores(1, n // 2, n, peak), axis=-1, keepdims=True)
    send_pair(1, shift, sums(1, shift))
    send_rows(1)
    loads["vu"].wait()
    loads["w"].wait()
    finish_rows(0)
    finish_rows(1)

    latent = lat_s[...].astype(BF16)
    up0 = jnp.dot(latent, vu_s[0], preferred_element_type=F32)
    up1 = jnp.dot(latent, vu_s[1], preferred_element_type=F32)
    values = jnp.concatenate([up0, pltpu.roll(up1, 6, 0)], axis=1)
    row8 = lax.broadcasted_iota(jnp.int32, values.shape, 0)
    values = jnp.where(row8 < 2, values, pltpu.roll(values, 6, 0)).astype(BF16)
    share = jnp.dot(values, w_s[...], preferred_element_type=F32)
    for j in range(NCHIP * NC):
        o_pair[j % NC, j // NC, :, pl.ds(0, DOUT)] = share[:4, j * DOUT:(j + 1) * DOUT]

    pair_out = pltpu.make_async_remote_copy(
        src_ref=o_pair.at[1 - c], dst_ref=o_pair_recv,
        send_sem=op_ss, recv_sem=op_rs, device_id=sibling, device_id_type=MESH)
    pair_out.start()
    pair_out.wait_recv()
    o_send[...] = (o_pair[c] + o_pair_recv[...]).astype(BF16)

    def o_copy(d):
        return pltpu.make_async_remote_copy(
            src_ref=o_send.at[away_chip(d)], dst_ref=o_recv.at[chip],
            send_sem=o_ss, recv_sem=o_rs, device_id=away(d), device_id_type=MESH)

    o_all = pltpu.make_async_remote_copy(
        src_ref=o_send.at[pl.ds(0, NCHIP - 1)], dst_ref=o_recv.at[pl.ds(0, NCHIP - 1)],
        send_sem=o_ss, recv_sem=o_rs, device_id=sibling, device_id_type=MESH)
    for d in AWAY:
        o_copy(d).start()
    o_recv[chip] = o_send[chip]
    o_all.wait_recv()
    final = jnp.sum(o_recv[...].astype(F32), axis=0)
    for r in range(2):
        for q in range(2):
            at = 2 * r + q
            out_ref[r, pl.ds(q, 1), :] = final[at:at + 1, :DOUT]

    for r in range(2):
        ag_all(r).wait_send()
        relay_copy(r, c).wait_send()
        pair_copy(r).wait_send()
        rs_all(r).wait_send()
    pair_out.wait_send()
    o_all.wait_send()


def per_device(queries, key_absorb, latent_cache, page_order, lengths, kerple_scale, kerple_rate,
               value_up, output_weight):
    any_spec = pl.BlockSpec(memory_space=pl.ANY)
    dma = pltpu.SemaphoreType.DMA
    out = pl.pallas_call(
        kernel,
        out_shape=jax.ShapeDtypeStruct((2, 2, DOUT), F32),
        in_specs=[any_spec] * 9,
        out_specs=pl.BlockSpec(memory_space=pltpu.VMEM),
        scratch_shapes=[
            pltpu.VMEM((2, 2, 2, NOPE + ROPE), BF16),
            pltpu.VMEM((8, NOPE + ROPE), F32),
            pltpu.VMEM((2, NOPE, LAT), BF16),
            pltpu.VMEM((2, WIDE, SLOTS), BF16),
            pltpu.SMEM((2, SLOTS // PAGE), jnp.int32),
            pltpu.SMEM((2,), jnp.int32),
            pltpu.VMEM((1, 128), F32),
            pltpu.VMEM((1, 128), F32),
            pltpu.VMEM((2, LAT, VDIM), BF16),
            pltpu.VMEM((2 * VDIM, D), BF16),
            pltpu.VMEM((2, NCHIP, 4, WIDE), BF16),
            pltpu.VMEM((HALF, WIDE), F32),
            pltpu.VMEM((2, NC, HALF, WIDE), BF16),
            pltpu.VMEM((ROWS, SLOTS), F32),
            pltpu.VMEM((ROWS, LAT), F32),
            pltpu.VMEM((ROWS, 128), F32),
            pltpu.VMEM((ROWS, 128), F32),
            pltpu.VMEM((2, HALF, WIDE), BF16),
            pltpu.VMEM((2, HALF, WIDE), BF16),
            pltpu.VMEM((HALF, WIDE), F32),
            pltpu.VMEM((2, NCHIP, 4, WIDE), BF16),
            pltpu.VMEM((2, NCHIP, 4, WIDE), BF16),
            pltpu.VMEM((8, LAT), F32),
            pltpu.VMEM((NC, NCHIP, 4, 128), F32),
            pltpu.VMEM((NCHIP, 4, 128), F32),
            pltpu.VMEM((NCHIP, 4, 128), BF16),
            pltpu.VMEM((NCHIP, 4, 128), BF16),
            dma((10,)),
            dma((2,)), dma((2,)),
            dma((2,)), dma((2,)),
            dma((2,)), dma((2,)),
            dma((2,)), dma((2,)),
            dma, dma,
            dma, dma,
        ],
        compiler_params=pltpu.CompilerParams(
            collective_id=0, has_side_effects=True, vmem_limit_bytes=56 * 1024 * 1024),
    )(
        queries, key_absorb, jnp.swapaxes(latent_cache, 1, 2), page_order, lengths,
        kerple_scale.reshape(1, 128), kerple_rate.reshape(1, 128), value_up, output_weight,
    )
    return out.astype(BF16)


def solution(mesh):
    in_specs = (
        P("rep", None, "ctx", None),
        P("ctx", None, None),
        P("rep", "ctx", None),
        P("rep", "ctx"),
        P("rep"),
        P(),
        P(),
        P("ctx", None, None),
        P("ctx", None),
    )
    out_specs = P("rep", None, "ctx")
    return jax.shard_map(
        per_device, mesh=mesh, in_specs=in_specs, out_specs=out_specs, check_vma=False
    )
```

```python
import functools
import math

import jax
import jax.numpy as jnp
from jax import lax
from jax.experimental import pallas as pl
from jax.experimental.pallas import tpu as pltpu
from jax.sharding import PartitionSpec as P

MESH = pl.DeviceIdType.MESH
F32 = jnp.float32
BF16 = jnp.bfloat16

NX, NZ, NC = 4, 8, 2
LAT, ROPE, NOPE, VDIM = 512, 64, 128, 128
WIDE = 640
SLOTS = 4096
PAGE = 128
D = 7168
DOUT = D // (NX * NZ * NC)
ROWS = 256
HALF = ROWS // 2
NCHIP = NX * NZ
SIGMA = (NOPE + ROPE) ** -0.5
KAPPA = SIGMA * math.log2(math.e)
FLOOR = -1.0e30


def steps(slot):
    return slot % NX, (slot // NX + NZ - 1) % NZ


def hops(slot):
    dx, dz = steps(slot)
    return min(dx, NX - dx) + min(dz, NZ - dz)


SELF = NX
AWAY = sorted((t for t in range(NCHIP) if t != SELF), key=lambda t: -hops(t))
FAR_FIRST_Z = (4, 3, 5, 2, 6, 1, 7, 0)
XCOLS = D // NX


def split3(v):
    hi = v.astype(BF16).astype(F32)
    rest = v - hi
    mid = rest.astype(BF16).astype(F32)
    return hi, mid, rest - mid


def pack_stats(c, l):
    lane = lax.broadcasted_iota(jnp.int32, c.shape, c.ndim - 1)
    out = jnp.zeros_like(c)
    for i, part in enumerate(split3(c) + split3(l)):
        out = jnp.where(lane == i, part, out)
    return out


def unpack_stats(st):
    lane = lax.broadcasted_iota(jnp.int32, st.shape, st.ndim - 1)
    c = jnp.sum(jnp.where(lane < 3, st, 0.0), axis=-1, keepdims=True)
    l = jnp.sum(jnp.where((lane >= 3) & (lane < 6), st, 0.0), axis=-1, keepdims=True)
    return c, l


def kernel(
    q_hbm, ka_hbm, kt_hbm, page_hbm, len_hbm, scale_hbm, rate_hbm, vu_hbm, w_hbm,
    out_ref,
    q_s, x_s, ka_s, kt_s, page_s, len_s, scale_s, rate_s, vu_s, w_s,
    qin, qf, qall, s_buf, rate_b, scale_b,
    pair_send, pair_recv, rs_f, rs_send, rs_recv, lat_s, o_pair, o_pair_recv, o_send, o_recv,
    local_sem, ag_ss, ag_rs, relay_ss, relay_rs, pair_ss, pair_rs, rs_ss, rs_rs,
    op_ss, op_rs, o_ss, o_rs,
):
    ctx = lax.axis_index("ctx")
    rep = lax.axis_index("rep")
    chip, c = ctx // NC, ctx % NC
    x, z = chip // NZ, chip % NZ
    sibling = (chip * NC + 1 - c, rep)

    def device(dx, dz):
        return ((((x + dx) % NX) * NZ + (z + dz) % NZ) * NC + c, rep)

    def toward(t):
        dx, dz = steps(t)
        return device(dx, dz)

    def back(t):
        dx, dz = steps(t)
        return device(NX - dx, NZ - dz)

    barrier = pltpu.get_barrier_semaphore()
    for t in AWAY:
        pl.semaphore_signal(barrier, inc=1, device_id=toward(t), device_id_type=MESH)
    pl.semaphore_signal(barrier, inc=1, device_id=sibling, device_id_type=MESH)

    loads = {
        name: pltpu.make_async_copy(src, dst, local_sem.at[i])
        for i, (name, src, dst) in enumerate((
            ("q", q_hbm, q_s),
            ("ka", ka_hbm, ka_s),
            ("scale", scale_hbm, scale_s),
            ("rate", rate_hbm, rate_s),
            ("page", page_hbm, page_s),
            ("len", len_hbm, len_s),
            ("k0", kt_hbm.at[0], kt_s.at[0, pl.ds(0, LAT + ROPE)]),
            ("k1", kt_hbm.at[1], kt_s.at[1, pl.ds(0, LAT + ROPE)]),
            ("vu", vu_hbm, vu_s),
            ("w", w_hbm, w_s),
        ))
    }
    for load in loads.values():
        load.start()

    loads["q"].wait()
    for r in range(2):
        for q in range(2):
            for hh in range(2):
                x_s[pl.ds(4 * r + 2 * hh + q, 1), :] = q_s[r, q, pl.ds(hh, 1), :].astype(F32)
    loads["ka"].wait()
    xq = x_s[...]
    nope = xq[:, :NOPE].astype(BF16)
    lat0 = jnp.dot(nope, ka_s[0], preferred_element_type=F32)
    lat1 = jnp.dot(nope, ka_s[1], preferred_element_type=F32)
    row8 = lax.broadcasted_iota(jnp.int32, (8, LAT), 0)
    lat = jnp.where((row8 // 2) % 2 == 0, lat0, lat1)
    for r in range(2):
        qin[r, SELF, :, pl.ds(0, LAT)] = lat[4 * r:4 * r + 4].astype(BF16)
        qin[r, SELF, :, pl.ds(LAT, 128)] = jnp.zeros((4, 128), BF16)
        qin[r, SELF, :, pl.ds(LAT, ROPE)] = xq[4 * r:4 * r + 4, NOPE:].astype(BF16)

    pl.semaphore_wait(barrier, len(AWAY) + 1)

    def ag_copy(r, t):
        return pltpu.make_async_remote_copy(
            src_ref=qin.at[r, SELF], dst_ref=qin.at[r, t],
            send_sem=ag_ss.at[r, t // 16], recv_sem=ag_rs.at[r, t // 16],
            device_id=toward(t), device_id_type=MESH)

    def ag_all(r, b):
        some = qin.at[r, pl.ds(0, 15 if b == 0 else 16)]
        return pltpu.make_async_remote_copy(
            src_ref=some, dst_ref=some, send_sem=ag_ss.at[r, b], recv_sem=ag_rs.at[r, b],
            device_id=sibling, device_id_type=MESH)

    for b in range(2):
        for r in range(2):
            for t in AWAY:
                if t // 16 == b:
                    ag_copy(r, t).start()

    for r in range(2):
        kt_s[r, pl.ds(LAT + ROPE, 64), :] = jnp.zeros((64, SLOTS), BF16)
    o_pair[...] = jnp.zeros_like(o_pair)
    row = lax.broadcasted_iota(jnp.int32, (ROWS, 128), 0)
    lane = lax.broadcasted_iota(jnp.int32, (ROWS, 128), 1)
    slot = (row // 128) * 16 + (row // 4) % 16
    from_x = (x + NX - slot % NX) % NX
    from_z = (z + 2 * NZ - (slot // NX + NZ - 1)) % NZ
    core = (c + (row // 64) % 2) % NC
    head = ((from_x * NZ + from_z) * NC + core) * 2 + (row // 2) % 2
    hot = lane == head
    loads["scale"].wait()
    loads["rate"].wait()
    rate_col = jnp.sum(jnp.where(hot, rate_s[...], 0.0), axis=-1, keepdims=True)
    scale_col = jnp.sum(jnp.where(hot, scale_s[...], 0.0), axis=-1, keepdims=True)
    rate_b[...] = jnp.broadcast_to(rate_col, (ROWS, 128))
    scale_b[...] = jnp.broadcast_to(scale_col * (1.0 / SIGMA), (ROWS, 128))
    loads["page"].wait()
    loads["len"].wait()

    def relay_copy(r, b):
        return pltpu.make_async_remote_copy(
            src_ref=qall.at[r, b, 0], dst_ref=qall.at[r, b, 1],
            send_sem=relay_ss.at[r, b], recv_sem=relay_rs.at[r, b],
            device_id=sibling, device_id_type=MESH)

    def relay(r, b):
        ag_all(r, b).wait_recv()
        for i in range(8):
            qf[pl.ds(8 * i, 4), :] = qin[r, 16 * b + 2 * i].astype(F32)
            qf[pl.ds(8 * i + 4, 4), :] = qin[r, 16 * b + 2 * i + 1].astype(F32)
        qall[r, b, 0] = qf[...].astype(BF16)
        relay_copy(r, b).start()

    sub8 = lax.broadcasted_iota(jnp.int32, (8, 128), 0)
    lane8 = lax.broadcasted_iota(jnp.int32, (8, 128), 1)
    offset = (sub8 % 2 - lane8).astype(F32)

    def scores(r, b):
        relay_copy(r, b).wait_recv()
        rows = pl.ds(HALF * b, HALF)
        rate = rate_b[rows, :].reshape(16, 8, 128)
        scale = scale_b[rows, :].reshape(16, 8, 128)
        base = len_s[r] - 2
        s = jnp.dot(qall[r, b].reshape(HALF, WIDE), kt_s[r], preferred_element_type=F32)
        peak = jnp.full((16, 8, 128), FLOOR, F32)
        for p in range(SLOTS // PAGE):
            dist = (base - page_s[r, p] * PAGE).astype(F32) + offset
            dist = jnp.where(dist >= 0.0, dist, jnp.inf)
            bias = scale * jnp.log(1.0 + rate * dist[None])
            u = s[:, p * PAGE:(p + 1) * PAGE].reshape(16, 8, 128) - bias
            s_buf[r, rows, pl.ds(p * PAGE, PAGE)] = u.reshape(HALF, 128)
            peak = jnp.maximum(peak, u)
        return jnp.max(peak, axis=-1, keepdims=True)

    def sums(r, near, far):
        shift = jnp.concatenate([near, far], axis=0)
        total = jnp.zeros((32, 8, 128), F32)
        weights = []
        for p in range(SLOTS // PAGE):
            u = s_buf[r, :, pl.ds(p * PAGE, PAGE)].reshape(32, 8, 128)
            w = jnp.exp2(KAPPA * (u - shift))
            total = total + w
            weights.append(w.reshape(ROWS, 128).astype(BF16))
        summed = lax.dot_general(
            jnp.concatenate(weights, axis=1), kt_s[r, pl.ds(0, LAT), :],
            (((1,), (1,)), ((), ())), preferred_element_type=F32)
        return shift, jnp.sum(total, axis=-1, keepdims=True), summed

    def pair_copy(r):
        return pltpu.make_async_remote_copy(
            src_ref=pair_send.at[r], dst_ref=pair_recv.at[r],
            send_sem=pair_ss.at[r], recv_sem=pair_rs.at[r],
            device_id=sibling, device_id_type=MESH)

    def send_pair(r, shift, total, summed):
        stats = pack_stats(
            jnp.broadcast_to(shift, (32, 8, 128)), jnp.broadcast_to(total, (32, 8, 128)))
        stats = stats.reshape(2, 2, 64, 128)
        summed = summed.reshape(2, 2, 64, LAT)
        for b in range(2):
            rows = pl.ds(64 * b, 64)
            pair_send[r, rows, pl.ds(0, LAT)] = summed[b, 1].astype(BF16)
            pair_send[r, rows, pl.ds(LAT, 128)] = stats[b, 1].astype(BF16)
        pair_copy(r).start()
        for b in range(2):
            rows = pl.ds(64 * b, 64)
            rs_f[rows, pl.ds(0, LAT)] = summed[b, 0]
            rs_f[rows, pl.ds(LAT, 128)] = stats[b, 0]

    def rs_copy(r, t):
        return pltpu.make_async_remote_copy(
            src_ref=rs_send.at[r, t], dst_ref=rs_recv.at[r, t],
            send_sem=rs_ss.at[r], recv_sem=rs_rs.at[r],
            device_id=back(t), device_id_type=MESH)

    def rs_all(r):
        return pltpu.make_async_remote_copy(
            src_ref=rs_send.at[r, pl.ds(0, NCHIP - 1)], dst_ref=rs_recv.at[r, pl.ds(0, NCHIP - 1)],
            send_sem=rs_ss.at[r], recv_sem=rs_rs.at[r],
            device_id=sibling, device_id_type=MESH)

    def send_rows(r):
        pair_copy(r).wait_recv()
        mine = rs_f[...].reshape(16, 8, WIDE)
        theirs = pair_recv[r].astype(F32).reshape(16, 8, WIDE)
        (c0, l0), (c1, l1) = unpack_stats(mine[..., LAT:]), unpack_stats(theirs[..., LAT:])
        shift = jnp.maximum(c0, c1)
        f0, f1 = jnp.exp2(KAPPA * (c0 - shift)), jnp.exp2(KAPPA * (c1 - shift))
        both = mine[..., :LAT] * f0 + theirs[..., :LAT] * f1
        stats = pack_stats(
            jnp.broadcast_to(shift, (16, 8, 128)), jnp.broadcast_to(l0 * f0 + l1 * f1, (16, 8, 128)))
        for i in range(NCHIP // 2):
            for h in range(2):
                rs_send[r, 2 * i + h, :, pl.ds(0, LAT)] = both[i, 4 * h:4 * h + 4].astype(BF16)
                rs_send[r, 2 * i + h, :, pl.ds(LAT, 128)] = stats[i, 4 * h:4 * h + 4].astype(BF16)
        for t in AWAY:
            rs_copy(r, t).start()
        rs_recv[r, SELF] = rs_send[r, SELF]

    def finish_rows(r):
        rs_all(r).wait_recv()
        parts = rs_recv[r].astype(F32)
        ci, li = unpack_stats(parts[..., LAT:])
        f = jnp.exp2(KAPPA * (ci - jnp.max(ci, axis=0, keepdims=True)))
        total = jnp.sum(parts[..., :LAT] * f, axis=0)
        lat_s[pl.ds(4 * r, 4), :] = total / jnp.sum(li * f, axis=0)

    relay(0, 0)
    relay(1, 0)
    loads["k0"].wait()
    near0 = scores(0, 0)
    loads["k1"].wait()
    near1 = scores(1, 0)
    relay(0, 1)
    far0 = scores(0, 1)
    relay(1, 1)
    send_pair(0, *sums(0, near0, far0))
    far1 = scores(1, 1)
    send_rows(0)
    send_pair(1, *sums(1, near1, far1))
    send_rows(1)
    loads["vu"].wait()
    loads["w"].wait()
    finish_rows(0)
    finish_rows(1)

    latent = lat_s[...].astype(BF16)
    up0 = jnp.dot(latent, vu_s[0], preferred_element_type=F32)
    up1 = jnp.dot(latent, vu_s[1], preferred_element_type=F32)
    values = jnp.concatenate([up0, pltpu.roll(up1, 6, 0)], axis=1)
    row8 = lax.broadcasted_iota(jnp.int32, values.shape, 0)
    values = jnp.where(row8 < 2, values, pltpu.roll(values, 6, 0)).astype(BF16)

    def out_pair(g):
        return pltpu.make_async_remote_copy(
            src_ref=o_pair.at[g, 1 - c], dst_ref=o_pair_recv.at[g],
            send_sem=op_ss.at[g], recv_sem=op_rs.at[g],
            device_id=sibling, device_id_type=MESH)

    def o_copy(g, dz):
        return pltpu.make_async_remote_copy(
            src_ref=o_send.at[g, (z + dz) % NZ], dst_ref=o_recv.at[g, dz],
            send_sem=o_ss.at[g], recv_sem=o_rs.at[g],
            device_id=device(g, dz), device_id_type=MESH)

    def o_all(g):
        some = pl.ds(0, 8 if g else 7)
        return pltpu.make_async_remote_copy(
            src_ref=o_send.at[g, some], dst_ref=o_recv.at[g, some],
            send_sem=o_ss.at[g], recv_sem=o_rs.at[g],
            device_id=sibling, device_id_type=MESH)

    def project(g):
        cols = pl.ds(pl.multiple_of(((x + g) % NX) * XCOLS, XCOLS), XCOLS)
        share = jnp.dot(values, w_s[:, cols], preferred_element_type=F32)
        for j in range(NZ * NC):
            o_pair[g, j % NC, j // NC, :, pl.ds(0, DOUT)] = share[:4, j * DOUT:(j + 1) * DOUT]
        out_pair(g).start()

    def send_columns(g):
        out_pair(g).wait_recv()
        o_send[g] = (o_pair[g, c] + o_pair_recv[g]).astype(BF16)
        for dz in FAR_FIRST_Z:
            if g or dz:
                o_copy(g, dz).start()

    order = (2, 1, 3, 0)
    for g in order:
        project(g)
    for g in order:
        send_columns(g)
    o_recv[0, 0] = o_send[0, z]
    for g in range(NX):
        o_all(g).wait_recv()
    final = jnp.sum(o_recv[...].reshape(NCHIP, 4, 128).astype(F32), axis=0)
    for r in range(2):
        for q in range(2):
            at = 2 * r + q
            out_ref[r, pl.ds(q, 1), :] = final[at:at + 1, :DOUT]

    for r in range(2):
        for b in range(2):
            ag_all(r, b).wait_send()
            relay_copy(r, b).wait_send()
        pair_copy(r).wait_send()
        rs_all(r).wait_send()
    for g in range(NX):
        out_pair(g).wait_send()
        o_all(g).wait_send()


def per_device(queries, key_absorb, latent_cache, page_order, lengths, kerple_scale, kerple_rate,
               value_up, output_weight):
    any_spec = pl.BlockSpec(memory_space=pl.ANY)
    dma = pltpu.SemaphoreType.DMA
    out = pl.pallas_call(
        kernel,
        out_shape=jax.ShapeDtypeStruct((2, 2, DOUT), F32),
        in_specs=[any_spec] * 9,
        out_specs=pl.BlockSpec(memory_space=pltpu.VMEM),
        scratch_shapes=[
            pltpu.VMEM((2, 2, 2, NOPE + ROPE), BF16),
            pltpu.VMEM((8, NOPE + ROPE), F32),
            pltpu.VMEM((2, NOPE, LAT), BF16),
            pltpu.VMEM((2, WIDE, SLOTS), BF16),
            pltpu.SMEM((2, SLOTS // PAGE), jnp.int32),
            pltpu.SMEM((2,), jnp.int32),
            pltpu.VMEM((1, 128), F32),
            pltpu.VMEM((1, 128), F32),
            pltpu.VMEM((2, LAT, VDIM), BF16),
            pltpu.VMEM((2 * VDIM, D), BF16),
            pltpu.VMEM((2, NCHIP, 4, WIDE), BF16),
            pltpu.VMEM((64, WIDE), F32),
            pltpu.VMEM((2, 2, 2, 64, WIDE), BF16),
            pltpu.VMEM((2, ROWS, SLOTS), F32),
            pltpu.VMEM((ROWS, 128), F32),
            pltpu.VMEM((ROWS, 128), F32),
            pltpu.VMEM((2, HALF, WIDE), BF16),
            pltpu.VMEM((2, HALF, WIDE), BF16),
            pltpu.VMEM((HALF, WIDE), F32),
            pltpu.VMEM((2, NCHIP, 4, WIDE), BF16),
            pltpu.VMEM((2, NCHIP, 4, WIDE), BF16),
            pltpu.VMEM((8, LAT), F32),
            pltpu.VMEM((NX, NC, NZ, 4, 128), F32),
            pltpu.VMEM((NX, NZ, 4, 128), F32),
            pltpu.VMEM((NX, NZ, 4, 128), BF16),
            pltpu.VMEM((NX, NZ, 4, 128), BF16),
            dma((10,)),
            dma((2, 2)), dma((2, 2)),
            dma((2, 2)), dma((2, 2)),
            dma((2,)), dma((2,)),
            dma((2,)), dma((2,)),
            dma((NX,)), dma((NX,)),
            dma((NX,)), dma((NX,)),
        ],
        compiler_params=pltpu.CompilerParams(
            collective_id=0, has_side_effects=True, vmem_limit_bytes=56 * 1024 * 1024),
    )(
        queries, key_absorb, jnp.swapaxes(latent_cache, 1, 2), page_order, lengths,
        kerple_scale.reshape(1, 128), kerple_rate.reshape(1, 128), value_up, output_weight,
    )
    return out.astype(BF16)


def solution(mesh):
    in_specs = (
        P("rep", None, "ctx", None),
        P("ctx", None, None),
        P("rep", "ctx", None),
        P("rep", "ctx"),
        P("rep"),
        P(),
        P(),
        P("ctx", None, None),
        P("ctx", None),
    )
    out_specs = P("rep", None, "ctx")
    return jax.shard_map(
        per_device, mesh=mesh, in_specs=in_specs, out_specs=out_specs, check_vma=False
    )
```

```python
import functools
import math

import jax
import jax.numpy as jnp
from jax import lax
from jax.experimental import pallas as pl
from jax.experimental.pallas import tpu as pltpu
from jax.sharding import PartitionSpec as P

MESH = pl.DeviceIdType.MESH
F32 = jnp.float32
BF16 = jnp.bfloat16

NX, NZ, NC = 4, 8, 2
LAT, ROPE, NOPE, VDIM = 512, 64, 128, 128
WIDE = 640
SLOTS = 4096
PAGE = 128
D = 7168
DOUT = D // (NX * NZ * NC)
ROWS = 256
HALF = ROWS // 2
NCHIP = NX * NZ
SIGMA = (NOPE + ROPE) ** -0.5
KAPPA = SIGMA * math.log2(math.e)
FLOOR = -1.0e30


def steps(slot):
    return slot % NX, (slot // NX + NZ - 1) % NZ


def hops(slot):
    dx, dz = steps(slot)
    return min(dx, NX - dx) + min(dz, NZ - dz)


SELF = NX
AWAY = sorted((t for t in range(NCHIP) if t != SELF), key=lambda t: -hops(t))
FAR_FIRST_Z = (4, 3, 5, 2, 6, 1, 7, 0)
XCOLS = D // NX


def split3(v):
    hi = v.astype(BF16).astype(F32)
    rest = v - hi
    mid = rest.astype(BF16).astype(F32)
    return hi, mid, rest - mid


def pack_stats(c, l):
    lane = lax.broadcasted_iota(jnp.int32, c.shape, c.ndim - 1)
    out = jnp.zeros_like(c)
    for i, part in enumerate(split3(c) + split3(l)):
        out = jnp.where(lane == i, part, out)
    return out


def unpack_stats(st):
    lane = lax.broadcasted_iota(jnp.int32, st.shape, st.ndim - 1)
    c = jnp.sum(jnp.where(lane < 3, st, 0.0), axis=-1, keepdims=True)
    l = jnp.sum(jnp.where((lane >= 3) & (lane < 6), st, 0.0), axis=-1, keepdims=True)
    return c, l


def kernel(
    q_hbm, ka_hbm, kt_hbm, page_hbm, len_hbm, scale_hbm, rate_hbm, vu_hbm, w_hbm,
    out_ref,
    q_s, x_s, ka_s, kt_s, page_s, len_s, scale_s, rate_s, vu_s, w_s,
    qin, qf, qall, s_buf, rate_b, scale_b,
    v_s, pair_send, pair_recv, rs_send, rs_recv, lat_s, o_send, o_recv,
    local_sem, ag_ss, ag_rs, relay_ss, relay_rs, pair_ss, pair_rs, rs_ss, rs_rs,
    o_ss, o_rs,
):
    ctx = lax.axis_index("ctx")
    rep = lax.axis_index("rep")
    chip, c = ctx // NC, ctx % NC
    x, z = chip // NZ, chip % NZ
    sibling = (chip * NC + 1 - c, rep)

    def device(dx, dz):
        return ((((x + dx) % NX) * NZ + (z + dz) % NZ) * NC + c, rep)

    def toward(t):
        dx, dz = steps(t)
        return device(dx, dz)

    def back(t):
        dx, dz = steps(t)
        return device(NX - dx, NZ - dz)

    barrier = pltpu.get_barrier_semaphore()
    for t in AWAY:
        pl.semaphore_signal(barrier, inc=1, device_id=toward(t), device_id_type=MESH)
    pl.semaphore_signal(barrier, inc=1, device_id=sibling, device_id_type=MESH)

    loads = {
        name: pltpu.make_async_copy(src, dst, local_sem.at[i])
        for i, (name, src, dst) in enumerate((
            ("q", q_hbm, q_s),
            ("ka", ka_hbm, ka_s),
            ("scale", scale_hbm, scale_s),
            ("rate", rate_hbm, rate_s),
            ("page", page_hbm, page_s),
            ("len", len_hbm, len_s),
            ("k0", kt_hbm.at[0], kt_s.at[0, pl.ds(0, LAT + ROPE)]),
            ("k1", kt_hbm.at[1], kt_s.at[1, pl.ds(0, LAT + ROPE)]),
            ("vu", vu_hbm, vu_s),
            ("w", w_hbm, w_s),
        ))
    }
    for load in loads.values():
        load.start()

    loads["q"].wait()
    for r in range(2):
        for q in range(2):
            for hh in range(2):
                x_s[pl.ds(4 * r + 2 * hh + q, 1), :] = q_s[r, q, pl.ds(hh, 1), :].astype(F32)
    loads["ka"].wait()
    xq = x_s[...]
    nope = xq[:, :NOPE].astype(BF16)
    lat0 = jnp.dot(nope, ka_s[0], preferred_element_type=F32)
    lat1 = jnp.dot(nope, ka_s[1], preferred_element_type=F32)
    row8 = lax.broadcasted_iota(jnp.int32, (8, LAT), 0)
    lat = jnp.where((row8 // 2) % 2 == 0, lat0, lat1)
    for r in range(2):
        qin[r, SELF, :, pl.ds(0, LAT)] = lat[4 * r:4 * r + 4].astype(BF16)
        qin[r, SELF, :, pl.ds(LAT, 128)] = jnp.zeros((4, 128), BF16)
        qin[r, SELF, :, pl.ds(LAT, ROPE)] = xq[4 * r:4 * r + 4, NOPE:].astype(BF16)

    pl.semaphore_wait(barrier, len(AWAY) + 1)

    def ag_copy(r, t):
        return pltpu.make_async_remote_copy(
            src_ref=qin.at[r, SELF], dst_ref=qin.at[r, t],
            send_sem=ag_ss.at[r, t // 16], recv_sem=ag_rs.at[r, t // 16],
            device_id=toward(t), device_id_type=MESH)

    def ag_all(r, b):
        some = qin.at[r, pl.ds(0, 15 if b == 0 else 16)]
        return pltpu.make_async_remote_copy(
            src_ref=some, dst_ref=some, send_sem=ag_ss.at[r, b], recv_sem=ag_rs.at[r, b],
            device_id=sibling, device_id_type=MESH)

    for r in range(2):
        for b in range(2):
            for t in AWAY:
                if t // 16 == b:
                    ag_copy(r, t).start()

    for r in range(2):
        kt_s[r, pl.ds(LAT + ROPE, 64), :] = jnp.zeros((64, SLOTS), BF16)
    o_send[...] = jnp.zeros_like(o_send)
    row = lax.broadcasted_iota(jnp.int32, (ROWS, 128), 0)
    lane = lax.broadcasted_iota(jnp.int32, (ROWS, 128), 1)
    slot = (row // 128) * 16 + (row // 4) % 16
    from_x = (x + NX - slot % NX) % NX
    from_z = (z + 2 * NZ - (slot // NX + NZ - 1)) % NZ
    core = (c + (row // 64) % 2) % NC
    head = ((from_x * NZ + from_z) * NC + core) * 2 + (row // 2) % 2
    hot = lane == head
    loads["scale"].wait()
    loads["rate"].wait()
    rate_col = jnp.sum(jnp.where(hot, rate_s[...], 0.0), axis=-1, keepdims=True)
    scale_col = jnp.sum(jnp.where(hot, scale_s[...], 0.0), axis=-1, keepdims=True)
    rate_b[...] = jnp.broadcast_to(rate_col, (ROWS, 128))
    scale_b[...] = jnp.broadcast_to(scale_col * (1.0 / SIGMA), (ROWS, 128))
    loads["page"].wait()
    loads["len"].wait()
    for r in range(2):
        loads["k%d" % r].wait()
        for i in range(8):
            cols = pl.ds(i * (SLOTS // 8), SLOTS // 8)
            v_s[r, cols, :] = kt_s[r, pl.ds(0, LAT), cols].T

    def relay_copy(r, b):
        return pltpu.make_async_remote_copy(
            src_ref=qall.at[r, b, 0], dst_ref=qall.at[r, b, 1],
            send_sem=relay_ss.at[r, b], recv_sem=relay_rs.at[r, b],
            device_id=sibling, device_id_type=MESH)

    def relay(r, b):
        ag_all(r, b).wait_recv()
        for i in range(8):
            qf[pl.ds(8 * i, 4), :] = qin[r, 16 * b + 2 * i].astype(F32)
            qf[pl.ds(8 * i + 4, 4), :] = qin[r, 16 * b + 2 * i + 1].astype(F32)
        qall[r, b, 0] = qf[...].astype(BF16)
        relay_copy(r, b).start()

    sub8 = lax.broadcasted_iota(jnp.int32, (8, 128), 0)
    lane8 = lax.broadcasted_iota(jnp.int32, (8, 128), 1)
    offset = (sub8 % 2 - lane8).astype(F32)

    def scores(r, b):
        relay_copy(r, b).wait_recv()
        rows = pl.ds(HALF * b, HALF)
        rate = rate_b[rows, :].reshape(16, 8, 128)
        scale = scale_b[rows, :].reshape(16, 8, 128)
        base = len_s[r] - 2
        s = jnp.dot(qall[r, b].reshape(HALF, WIDE), kt_s[r], preferred_element_type=F32)
        peak = jnp.full((16, 8, 128), FLOOR, F32)
        for p in range(SLOTS // PAGE):
            dist = (base - page_s[r, p] * PAGE).astype(F32) + offset
            dist = jnp.where(dist >= 0.0, dist, jnp.inf)
            bias = scale * jnp.log(1.0 + rate * dist[None])
            u = s[:, p * PAGE:(p + 1) * PAGE].reshape(16, 8, 128) - bias
            s_buf[r, rows, pl.ds(p * PAGE, PAGE)] = u.reshape(HALF, 128)
            peak = jnp.maximum(peak, u)
        return jnp.max(peak, axis=-1, keepdims=True)

    def sums(r, b, shift):
        total = jnp.zeros((16, 8, 128), F32)
        weights = []
        for p in range(SLOTS // PAGE):
            u = s_buf[r, pl.ds(HALF * b, HALF), pl.ds(p * PAGE, PAGE)].reshape(16, 8, 128)
            w = jnp.exp2(KAPPA * (u - shift))
            total = total + w
            weights.append(w.reshape(HALF, 128).astype(BF16))
        summed = jnp.dot(jnp.concatenate(weights, axis=1), v_s[r], preferred_element_type=F32)
        return jnp.sum(total, axis=-1, keepdims=True), summed

    def pair_copy(r, b):
        return pltpu.make_async_remote_copy(
            src_ref=pair_send.at[r, b], dst_ref=pair_recv.at[r, b],
            send_sem=pair_ss.at[r, b], recv_sem=pair_rs.at[r, b],
            device_id=sibling, device_id_type=MESH)

    def attend(r, b, shift):
        total, summed = sums(r, b, shift)
        shift = jnp.broadcast_to(shift, (16, 8, 128))
        total = jnp.broadcast_to(total, (16, 8, 128))
        pair_send[r, b, :, pl.ds(0, LAT)] = summed[64:].astype(BF16)
        pair_send[r, b, :, pl.ds(LAT, 128)] = pack_stats(shift[8:], total[8:]).reshape(64, 128).astype(BF16)
        pair_copy(r, b).start()
        return shift[:8, :, :1], total[:8, :, :1], summed[:64].reshape(8, 8, LAT)

    def rs_copy(r, t):
        return pltpu.make_async_remote_copy(
            src_ref=rs_send.at[r, t], dst_ref=rs_recv.at[r, t],
            send_sem=rs_ss.at[r, t // 16], recv_sem=rs_rs.at[r, t // 16],
            device_id=back(t), device_id_type=MESH)

    def rs_all(r, b):
        some = pl.ds(0, 15 if b == 0 else 16)
        return pltpu.make_async_remote_copy(
            src_ref=rs_send.at[r, some], dst_ref=rs_recv.at[r, some],
            send_sem=rs_ss.at[r, b], recv_sem=rs_rs.at[r, b],
            device_id=sibling, device_id_type=MESH)

    def send_rows(r, b, own):
        c0, l0, mine = own
        pair_copy(r, b).wait_recv()
        theirs = pair_recv[r, b].astype(F32).reshape(8, 8, WIDE)
        c1, l1 = unpack_stats(theirs[..., LAT:])
        shift = jnp.maximum(c0, c1)
        f0, f1 = jnp.exp2(KAPPA * (c0 - shift)), jnp.exp2(KAPPA * (c1 - shift))
        both = mine * f0 + theirs[..., :LAT] * f1
        stats = pack_stats(
            jnp.broadcast_to(shift, (8, 8, 128)), jnp.broadcast_to(l0 * f0 + l1 * f1, (8, 8, 128)))
        for i in range(8):
            for h in range(2):
                t = 16 * b + 2 * i + h
                rs_send[r, t, :, pl.ds(0, LAT)] = both[i, 4 * h:4 * h + 4].astype(BF16)
                rs_send[r, t, :, pl.ds(LAT, 128)] = stats[i, 4 * h:4 * h + 4].astype(BF16)
        for t in AWAY:
            if t // 16 == b:
                rs_copy(r, t).start()
        if b == 0:
            rs_recv[r, SELF] = rs_send[r, SELF]

    def finish_rows(r):
        rs_all(r, 0).wait_recv()
        rs_all(r, 1).wait_recv()
        parts = rs_recv[r].astype(F32)
        ci, li = unpack_stats(parts[..., LAT:])
        f = jnp.exp2(KAPPA * (ci - jnp.max(ci, axis=0, keepdims=True)))
        total = jnp.sum(parts[..., :LAT] * f, axis=0)
        lat_s[pl.ds(4 * r, 4), :] = total / jnp.sum(li * f, axis=0)

    relay(0, 0)
    near0 = scores(0, 0)
    relay(0, 1)
    far0 = scores(0, 1)
    relay(1, 0)
    far0 = attend(0, 1, far0)
    near0 = attend(0, 0, near0)
    send_rows(0, 1, far0)
    near1 = scores(1, 0)
    relay(1, 1)
    send_rows(0, 0, near0)
    far1 = scores(1, 1)
    far1 = attend(1, 1, far1)
    near1 = attend(1, 0, near1)
    send_rows(1, 1, far1)
    send_rows(1, 0, near1)
    loads["vu"].wait()
    loads["w"].wait()
    finish_rows(0)
    finish_rows(1)

    latent = lat_s[...].astype(BF16)
    up0 = jnp.dot(latent, vu_s[0], preferred_element_type=F32)
    up1 = jnp.dot(latent, vu_s[1], preferred_element_type=F32)
    values = jnp.concatenate([up0, pltpu.roll(up1, 6, 0)], axis=1)
    row8 = lax.broadcasted_iota(jnp.int32, values.shape, 0)
    values = jnp.where(row8 < 2, values, pltpu.roll(values, 6, 0)).astype(BF16)

    def o_copy(g, dz, dc):
        zz, cc = (z + dz) % NZ, (c + dc) % NC
        return pltpu.make_async_remote_copy(
            src_ref=o_send.at[g, zz, cc], dst_ref=o_recv.at[g, dz, dc],
            send_sem=o_ss.at[g], recv_sem=o_rs.at[g],
            device_id=((((x + g) % NX) * NZ + zz) * NC + cc, rep), device_id_type=MESH)

    def o_all(g):
        some = pl.ds(0, 8 if g else 7)
        return pltpu.make_async_remote_copy(
            src_ref=o_send.at[g, some], dst_ref=o_recv.at[g, some],
            send_sem=o_ss.at[g], recv_sem=o_rs.at[g],
            device_id=sibling, device_id_type=MESH)

    def sib_copy():
        return pltpu.make_async_remote_copy(
            src_ref=o_send.at[0, z, 1 - c], dst_ref=o_recv.at[0, 0, 1],
            send_sem=o_ss.at[NX], recv_sem=o_rs.at[NX],
            device_id=sibling, device_id_type=MESH)

    for g in (2, 1, 3, 0):
        cols = pl.ds(pl.multiple_of(((x + g) % NX) * XCOLS, XCOLS), XCOLS)
        share = jnp.dot(values, w_s[:, cols], preferred_element_type=F32)
        for j in range(NZ * NC):
            o_send[g, j // NC, j % NC, :, pl.ds(0, DOUT)] = share[:4, j * DOUT:(j + 1) * DOUT].astype(BF16)
        for dz in FAR_FIRST_Z:
            if g or dz:
                for dc in range(NC):
                    o_copy(g, dz, dc).start()
    sib_copy().start()
    o_recv[0, 0, 0] = o_send[0, z, c]
    for g in (0, 1, 3, 2):
        o_all(g).wait_recv()
    sib_copy().wait_recv()
    final = jnp.sum(o_recv[...].reshape(NCHIP * NC, 4, 128).astype(F32), axis=0)
    for r in range(2):
        for q in range(2):
            at = 2 * r + q
            out_ref[r, pl.ds(q, 1), :] = final[at:at + 1, :DOUT]

    for r in range(2):
        for b in range(2):
            ag_all(r, b).wait_send()
            relay_copy(r, b).wait_send()
            pair_copy(r, b).wait_send()
            rs_all(r, b).wait_send()
    for g in range(NX):
        o_all(g).wait_send()
    sib_copy().wait_send()


def per_device(queries, key_absorb, latent_cache, page_order, lengths, kerple_scale, kerple_rate,
               value_up, output_weight):
    any_spec = pl.BlockSpec(memory_space=pl.ANY)
    dma = pltpu.SemaphoreType.DMA
    out = pl.pallas_call(
        kernel,
        out_shape=jax.ShapeDtypeStruct((2, 2, DOUT), F32),
        in_specs=[any_spec] * 9,
        out_specs=pl.BlockSpec(memory_space=pltpu.VMEM),
        scratch_shapes=[
            pltpu.VMEM((2, 2, 2, NOPE + ROPE), BF16),
            pltpu.VMEM((8, NOPE + ROPE), F32),
            pltpu.VMEM((2, NOPE, LAT), BF16),
            pltpu.VMEM((2, WIDE, SLOTS), BF16),
            pltpu.SMEM((2, SLOTS // PAGE), jnp.int32),
            pltpu.SMEM((2,), jnp.int32),
            pltpu.VMEM((1, 128), F32),
            pltpu.VMEM((1, 128), F32),
            pltpu.VMEM((2, LAT, VDIM), BF16),
            pltpu.VMEM((2 * VDIM, D), BF16),
            pltpu.VMEM((2, NCHIP, 4, WIDE), BF16),
            pltpu.VMEM((64, WIDE), F32),
            pltpu.VMEM((2, 2, 2, 64, WIDE), BF16),
            pltpu.VMEM((2, ROWS, SLOTS), F32),
            pltpu.VMEM((ROWS, 128), F32),
            pltpu.VMEM((ROWS, 128), F32),
            pltpu.VMEM((2, SLOTS, LAT), BF16),
            pltpu.VMEM((2, 2, 64, WIDE), BF16),
            pltpu.VMEM((2, 2, 64, WIDE), BF16),
            pltpu.VMEM((2, NCHIP, 4, WIDE), BF16),
            pltpu.VMEM((2, NCHIP, 4, WIDE), BF16),
            pltpu.VMEM((8, LAT), F32),
            pltpu.VMEM((NX, NZ, NC, 4, 128), BF16),
            pltpu.VMEM((NX, NZ, NC, 4, 128), BF16),
            dma((10,)),
            dma((2, 2)), dma((2, 2)),
            dma((2, 2)), dma((2, 2)),
            dma((2, 2)), dma((2, 2)),
            dma((2, 2)), dma((2, 2)),
            dma((NX + 1,)), dma((NX + 1,)),
        ],
        compiler_params=pltpu.CompilerParams(
            collective_id=0, has_side_effects=True, vmem_limit_bytes=56 * 1024 * 1024),
    )(
        queries, key_absorb, jnp.swapaxes(latent_cache, 1, 2), page_order, lengths,
        kerple_scale.reshape(1, 128), kerple_rate.reshape(1, 128), value_up, output_weight,
    )
    return out.astype(BF16)


def solution(mesh):
    in_specs = (
        P("rep", None, "ctx", None),
        P("ctx", None, None),
        P("rep", "ctx", None),
        P("rep", "ctx"),
        P("rep"),
        P(),
        P(),
        P("ctx", None, None),
        P("ctx", None),
    )
    out_specs = P("rep", None, "ctx")
    return jax.shard_map(
        per_device, mesh=mesh, in_specs=in_specs, out_specs=out_specs, check_vma=False
    )
```

```python
import functools
import math

import jax
import jax.numpy as jnp
from jax import lax
from jax.experimental import pallas as pl
from jax.experimental.pallas import tpu as pltpu
from jax.sharding import PartitionSpec as P

MESH = pl.DeviceIdType.MESH
F32 = jnp.float32
BF16 = jnp.bfloat16

NX, NZ, NC = 4, 8, 2
LAT, ROPE, NOPE, VDIM = 512, 64, 128, 128
WIDE = 640
SLOTS = 4096
PAGE = 128
D = 7168
DOUT = D // (NX * NZ * NC)
ROWS = 256
HALF = ROWS // 2
NCHIP = NX * NZ
SIGMA = (NOPE + ROPE) ** -0.5
KAPPA = SIGMA * math.log2(math.e)
FLOOR = -1.0e30


def steps(slot):
    return slot % NX, (slot // NX + NZ - 1) % NZ


def hops(slot):
    dx, dz = steps(slot)
    return min(dx, NX - dx) + min(dz, NZ - dz)


SELF = NX
AWAY = sorted((t for t in range(NCHIP) if t != SELF), key=lambda t: -hops(t))
FAR_FIRST_Z = (4, 3, 5, 2, 6, 1, 7, 0)
XCOLS = D // NX


def split3(v):
    hi = v.astype(BF16).astype(F32)
    rest = v - hi
    mid = rest.astype(BF16).astype(F32)
    return hi, mid, rest - mid


def pack_stats(c, l):
    lane = lax.broadcasted_iota(jnp.int32, c.shape, c.ndim - 1)
    out = jnp.zeros_like(c)
    for i, part in enumerate(split3(c) + split3(l)):
        out = jnp.where(lane == i, part, out)
    return out


def unpack_stats(st):
    lane = lax.broadcasted_iota(jnp.int32, st.shape, st.ndim - 1)
    c = jnp.sum(jnp.where(lane < 3, st, 0.0), axis=-1, keepdims=True)
    l = jnp.sum(jnp.where((lane >= 3) & (lane < 6), st, 0.0), axis=-1, keepdims=True)
    return c, l


def kernel(
    q_hbm, ka_hbm, kt_hbm, page_hbm, len_hbm, scale_hbm, rate_hbm, vu_hbm, w_hbm,
    out_ref,
    q_s, x_s, ka_s, kt_s, page_s, len_s, scale_s, rate_s, vu_s, w_s,
    qin0, qin1, qf, qall, s_buf, rate_b, scale_b,
    v_s, pair_send, pair_recv, rs_send, rs_recv, lat_s, o_send, o_recv,
    local_sem, ag_ss, ag_rs, relay_ss, relay_rs, pair_ss, pair_rs, rs_ss, rs_rs,
    o_ss, o_rs,
):
    ctx = lax.axis_index("ctx")
    rep = lax.axis_index("rep")
    chip, c = ctx // NC, ctx % NC
    x, z = chip // NZ, chip % NZ
    sibling = (chip * NC + 1 - c, rep)

    def device(dx, dz):
        return ((((x + dx) % NX) * NZ + (z + dz) % NZ) * NC + c, rep)

    def toward(t):
        dx, dz = steps(t)
        return device(dx, dz)

    def back(t):
        dx, dz = steps(t)
        return device(NX - dx, NZ - dz)

    barrier = pltpu.get_barrier_semaphore()
    for t in AWAY:
        pl.semaphore_signal(barrier, inc=1, device_id=toward(t), device_id_type=MESH)
    pl.semaphore_signal(barrier, inc=1, device_id=sibling, device_id_type=MESH)

    loads = {
        name: pltpu.make_async_copy(src, dst, local_sem.at[i])
        for i, (name, src, dst) in enumerate((
            ("q", q_hbm, q_s),
            ("ka", ka_hbm, ka_s),
            ("scale", scale_hbm, scale_s),
            ("rate", rate_hbm, rate_s),
            ("page", page_hbm, page_s),
            ("len", len_hbm, len_s),
            ("k0", kt_hbm.at[0], kt_s.at[0, pl.ds(0, LAT + ROPE)]),
            ("k1", kt_hbm.at[1, pl.ds(0, LAT)], kt_s.at[1, pl.ds(0, LAT)]),
            ("k1r", kt_hbm.at[1, pl.ds(LAT, ROPE)], kt_s.at[1, pl.ds(LAT + ROPE, ROPE)]),
            ("vu", vu_hbm, vu_s),
            ("w", w_hbm, w_s),
        ))
    }
    for name, load in loads.items():
        if name not in ("vu", "w"):
            load.start()

    loads["q"].wait()
    for r in range(2):
        for q in range(2):
            for hh in range(2):
                x_s[pl.ds(4 * r + 2 * hh + q, 1), :] = q_s[r, q, pl.ds(hh, 1), :].astype(F32)
    loads["ka"].wait()
    xq = x_s[...]
    nope = xq[:, :NOPE].astype(BF16)
    lat0 = jnp.dot(nope, ka_s[0], preferred_element_type=F32)
    lat1 = jnp.dot(nope, ka_s[1], preferred_element_type=F32)
    row8 = lax.broadcasted_iota(jnp.int32, (8, LAT), 0)
    lat = jnp.where((row8 // 2) % 2 == 0, lat0, lat1)
    qin0[SELF, :, pl.ds(0, LAT)] = lat[:4].astype(BF16)
    qin0[SELF, :, pl.ds(LAT, ROPE)] = xq[:4, NOPE:].astype(BF16)
    qin0[SELF, :, pl.ds(LAT + ROPE, ROPE)] = xq[4:, NOPE:].astype(BF16)
    qin1[SELF] = lat[4:].astype(BF16)

    kt_s[0, pl.ds(LAT + ROPE, ROPE), :] = jnp.zeros((ROPE, SLOTS), BF16)
    kt_s[1, pl.ds(LAT, ROPE), :] = jnp.zeros((ROPE, SLOTS), BF16)
    o_send[...] = jnp.zeros_like(o_send)
    row = lax.broadcasted_iota(jnp.int32, (ROWS, 128), 0)
    lane = lax.broadcasted_iota(jnp.int32, (ROWS, 128), 1)
    slot = (row // 128) * 16 + (row // 4) % 16
    from_x = (x + NX - slot % NX) % NX
    from_z = (z + 2 * NZ - (slot // NX + NZ - 1)) % NZ
    core = (c + (row // 64) % 2) % NC
    head = ((from_x * NZ + from_z) * NC + core) * 2 + (row // 2) % 2
    hot = lane == head
    loads["scale"].wait()
    loads["rate"].wait()
    rate_col = jnp.sum(jnp.where(hot, rate_s[...], 0.0), axis=-1, keepdims=True)
    scale_col = jnp.sum(jnp.where(hot, scale_s[...], 0.0), axis=-1, keepdims=True)
    rate_b[...] = jnp.broadcast_to(rate_col, (ROWS, 128))
    scale_b[...] = jnp.broadcast_to(scale_col * (1.0 / SIGMA), (ROWS, 128))
    loads["page"].wait()
    loads["len"].wait()

    def transpose(r):
        for i in range(8):
            cols = pl.ds(i * (SLOTS // 8), SLOTS // 8)
            v_s[r, cols, :] = kt_s[r, pl.ds(0, LAT), cols].T

    pl.semaphore_wait(barrier, len(AWAY) + 1)

    qin = (qin0, qin1)

    def ag_copy(r, t):
        return pltpu.make_async_remote_copy(
            src_ref=qin[r].at[SELF], dst_ref=qin[r].at[t],
            send_sem=ag_ss.at[r, t // 16], recv_sem=ag_rs.at[r, t // 16],
            device_id=toward(t), device_id_type=MESH)

    def ag_all(r, b):
        some = qin[r].at[pl.ds(0, 15 if b == 0 else 16)]
        return pltpu.make_async_remote_copy(
            src_ref=some, dst_ref=some, send_sem=ag_ss.at[r, b], recv_sem=ag_rs.at[r, b],
            device_id=sibling, device_id_type=MESH)

    for r, b in ((0, 0), (0, 1), (1, 1), (1, 0)):
        for t in AWAY:
            if t // 16 == b:
                ag_copy(r, t).start()


    loads["k0"].wait()
    transpose(0)
    loads["k1"].wait()
    loads["k1r"].wait()
    loads["vu"].start()
    loads["w"].start()
    transpose(1)

    def relay_copy(r, b):
        return pltpu.make_async_remote_copy(
            src_ref=qall.at[r, b, 0], dst_ref=qall.at[r, b, 1],
            send_sem=relay_ss.at[r, b], recv_sem=relay_rs.at[r, b],
            device_id=sibling, device_id_type=MESH)

    def relay(r, b):
        ag_all(r, b).wait_recv()
        for i in range(16):
            t, rows = 16 * b + i, pl.ds(4 * i, 4)
            if r == 0:
                qf[rows, :] = qin0[t].astype(F32)
            else:
                qf[rows, pl.ds(0, LAT)] = qin1[t].astype(F32)
                qf[rows, pl.ds(LAT, 128)] = qin0[t, :, pl.ds(LAT, 128)].astype(F32)
        qall[r, b, 0] = qf[...].astype(BF16)
        relay_copy(r, b).start()

    sub8 = lax.broadcasted_iota(jnp.int32, (8, 128), 0)
    lane8 = lax.broadcasted_iota(jnp.int32, (8, 128), 1)
    offset = (sub8 % 2 - lane8).astype(F32)

    def scores(r, b):
        relay_copy(r, b).wait_recv()
        rows = pl.ds(HALF * b, HALF)
        rate = rate_b[rows, :].reshape(16, 8, 128)
        scale = scale_b[rows, :].reshape(16, 8, 128)
        base = len_s[r] - 2
        s = jnp.dot(qall[r, b].reshape(HALF, WIDE), kt_s[r], preferred_element_type=F32)
        peak = jnp.full((16, 8, 128), FLOOR, F32)
        for p in range(SLOTS // PAGE):
            dist = (base - page_s[r, p] * PAGE).astype(F32) + offset
            dist = jnp.where(dist >= 0.0, dist, jnp.inf)
            bias = scale * jnp.log(1.0 + rate * dist[None])
            u = s[:, p * PAGE:(p + 1) * PAGE].reshape(16, 8, 128) - bias
            s_buf[r, rows, pl.ds(p * PAGE, PAGE)] = u.reshape(HALF, 128)
            peak = jnp.maximum(peak, u)
        return jnp.max(peak, axis=-1, keepdims=True)

    def sums(r, b, shift):
        total = jnp.zeros((16, 8, 128), F32)
        weights = []
        for p in range(SLOTS // PAGE):
            u = s_buf[r, pl.ds(HALF * b, HALF), pl.ds(p * PAGE, PAGE)].reshape(16, 8, 128)
            w = jnp.exp2(KAPPA * (u - shift))
            total = total + w
            weights.append(w.reshape(HALF, 128).astype(BF16))
        summed = jnp.dot(jnp.concatenate(weights, axis=1), v_s[r], preferred_element_type=F32)
        return jnp.sum(total, axis=-1, keepdims=True), summed

    def pair_copy(r, b):
        return pltpu.make_async_remote_copy(
            src_ref=pair_send.at[r, b], dst_ref=pair_recv.at[r, b],
            send_sem=pair_ss.at[r, b], recv_sem=pair_rs.at[r, b],
            device_id=sibling, device_id_type=MESH)

    def attend(r, b, shift):
        total, summed = sums(r, b, shift)
        shift = jnp.broadcast_to(shift, (16, 8, 128))
        total = jnp.broadcast_to(total, (16, 8, 128))
        pair_send[r, b, :, pl.ds(0, LAT)] = summed[64:].astype(BF16)
        pair_send[r, b, :, pl.ds(LAT, 128)] = pack_stats(shift[8:], total[8:]).reshape(64, 128).astype(BF16)
        pair_copy(r, b).start()
        return shift[:8, :, :1], total[:8, :, :1], summed[:64].reshape(8, 8, LAT)

    def rs_copy(r, t):
        return pltpu.make_async_remote_copy(
            src_ref=rs_send.at[r, t], dst_ref=rs_recv.at[r, t],
            send_sem=rs_ss.at[r, t // 16], recv_sem=rs_rs.at[r, t // 16],
            device_id=back(t), device_id_type=MESH)

    def rs_all(r, b):
        some = pl.ds(0, 15 if b == 0 else 16)
        return pltpu.make_async_remote_copy(
            src_ref=rs_send.at[r, some], dst_ref=rs_recv.at[r, some],
            send_sem=rs_ss.at[r, b], recv_sem=rs_rs.at[r, b],
            device_id=sibling, device_id_type=MESH)

    def send_rows(r, b, own):
        c0, l0, mine = own
        pair_copy(r, b).wait_recv()
        theirs = pair_recv[r, b].astype(F32).reshape(8, 8, WIDE)
        c1, l1 = unpack_stats(theirs[..., LAT:])
        shift = jnp.maximum(c0, c1)
        f0, f1 = jnp.exp2(KAPPA * (c0 - shift)), jnp.exp2(KAPPA * (c1 - shift))
        both = mine * f0 + theirs[..., :LAT] * f1
        stats = pack_stats(
            jnp.broadcast_to(shift, (8, 8, 128)), jnp.broadcast_to(l0 * f0 + l1 * f1, (8, 8, 128)))
        for i in range(8):
            for h in range(2):
                t = 16 * b + 2 * i + h
                rs_send[r, t, :, pl.ds(0, LAT)] = both[i, 4 * h:4 * h + 4].astype(BF16)
                rs_send[r, t, :, pl.ds(LAT, 128)] = stats[i, 4 * h:4 * h + 4].astype(BF16)
        for t in AWAY:
            if t // 16 == b:
                rs_copy(r, t).start()
        if b == 0:
            rs_recv[r, SELF] = rs_send[r, SELF]

    def finish_rows(r):
        rs_all(r, 0).wait_recv()
        rs_all(r, 1).wait_recv()
        parts = rs_recv[r].astype(F32)
        ci, li = unpack_stats(parts[..., LAT:])
        f = jnp.exp2(KAPPA * (ci - jnp.max(ci, axis=0, keepdims=True)))
        total = jnp.sum(parts[..., :LAT] * f, axis=0)
        lat_s[pl.ds(4 * r, 4), :] = total / jnp.sum(li * f, axis=0)

    relay(0, 0)
    near0 = scores(0, 0)
    relay(0, 1)
    near0 = attend(0, 0, near0)
    far0 = scores(0, 1)
    relay(1, 1)
    far0 = attend(0, 1, far0)
    send_rows(0, 0, near0)
    far1 = scores(1, 1)
    relay(1, 0)
    send_rows(0, 1, far0)
    far1 = attend(1, 1, far1)
    near1 = scores(1, 0)
    send_rows(1, 1, far1)
    near1 = attend(1, 0, near1)
    send_rows(1, 0, near1)
    loads["vu"].wait()
    loads["w"].wait()
    finish_rows(0)
    finish_rows(1)

    latent = lat_s[...].astype(BF16)
    up0 = jnp.dot(latent, vu_s[0], preferred_element_type=F32)
    up1 = jnp.dot(latent, vu_s[1], preferred_element_type=F32)
    values = jnp.concatenate([up0, pltpu.roll(up1, 6, 0)], axis=1)
    row8 = lax.broadcasted_iota(jnp.int32, values.shape, 0)
    values = jnp.where(row8 < 2, values, pltpu.roll(values, 6, 0)).astype(BF16)

    def o_copy(g, dz, dc):
        zz, cc = (z + dz) % NZ, (c + dc) % NC
        return pltpu.make_async_remote_copy(
            src_ref=o_send.at[g, zz, cc], dst_ref=o_recv.at[g, dz, dc],
            send_sem=o_ss.at[g], recv_sem=o_rs.at[g],
            device_id=((((x + g) % NX) * NZ + zz) * NC + cc, rep), device_id_type=MESH)

    def o_all(g):
        some = pl.ds(0, 8 if g else 7)
        return pltpu.make_async_remote_copy(
            src_ref=o_send.at[g, some], dst_ref=o_recv.at[g, some],
            send_sem=o_ss.at[g], recv_sem=o_rs.at[g],
            device_id=sibling, device_id_type=MESH)

    def sib_copy():
        return pltpu.make_async_remote_copy(
            src_ref=o_send.at[0, z, 1 - c], dst_ref=o_recv.at[0, 0, 1],
            send_sem=o_ss.at[NX], recv_sem=o_rs.at[NX],
            device_id=sibling, device_id_type=MESH)

    for g in (2, 1, 3, 0):
        cols = pl.ds(pl.multiple_of(((x + g) % NX) * XCOLS, XCOLS), XCOLS)
        share = jnp.dot(values, w_s[:, cols], preferred_element_type=F32)
        for j in range(NZ * NC):
            o_send[g, j // NC, j % NC, :, pl.ds(0, DOUT)] = share[:4, j * DOUT:(j + 1) * DOUT].astype(BF16)
        for dz in FAR_FIRST_Z:
            if g or dz:
                for dc in range(NC):
                    o_copy(g, dz, dc).start()
    sib_copy().start()
    o_recv[0, 0, 0] = o_send[0, z, c]
    for g in (0, 1, 3, 2):
        o_all(g).wait_recv()
    sib_copy().wait_recv()
    final = jnp.sum(o_recv[...].reshape(NCHIP * NC, 4, 128).astype(F32), axis=0)
    for r in range(2):
        for q in range(2):
            at = 2 * r + q
            out_ref[r, pl.ds(q, 1), :] = final[at:at + 1, :DOUT]

    for r in range(2):
        for b in range(2):
            ag_all(r, b).wait_send()
            relay_copy(r, b).wait_send()
            pair_copy(r, b).wait_send()
            rs_all(r, b).wait_send()
    for g in range(NX):
        o_all(g).wait_send()
    sib_copy().wait_send()


def per_device(queries, key_absorb, latent_cache, page_order, lengths, kerple_scale, kerple_rate,
               value_up, output_weight):
    any_spec = pl.BlockSpec(memory_space=pl.ANY)
    dma = pltpu.SemaphoreType.DMA
    out = pl.pallas_call(
        kernel,
        out_shape=jax.ShapeDtypeStruct((2, 2, DOUT), F32),
        in_specs=[any_spec] * 9,
        out_specs=pl.BlockSpec(memory_space=pltpu.VMEM),
        scratch_shapes=[
            pltpu.VMEM((2, 2, 2, NOPE + ROPE), BF16),
            pltpu.VMEM((8, NOPE + ROPE), F32),
            pltpu.VMEM((2, NOPE, LAT), BF16),
            pltpu.VMEM((2, WIDE, SLOTS), BF16),
            pltpu.SMEM((2, SLOTS // PAGE), jnp.int32),
            pltpu.SMEM((2,), jnp.int32),
            pltpu.VMEM((1, 128), F32),
            pltpu.VMEM((1, 128), F32),
            pltpu.VMEM((2, LAT, VDIM), BF16),
            pltpu.VMEM((2 * VDIM, D), BF16),
            pltpu.VMEM((NCHIP, 4, WIDE), BF16),
            pltpu.VMEM((NCHIP, 4, LAT), BF16),
            pltpu.VMEM((64, WIDE), F32),
            pltpu.VMEM((2, 2, 2, 64, WIDE), BF16),
            pltpu.VMEM((2, ROWS, SLOTS), F32),
            pltpu.VMEM((ROWS, 128), F32),
            pltpu.VMEM((ROWS, 128), F32),
            pltpu.VMEM((2, SLOTS, LAT), BF16),
            pltpu.VMEM((2, 2, 64, WIDE), BF16),
            pltpu.VMEM((2, 2, 64, WIDE), BF16),
            pltpu.VMEM((2, NCHIP, 4, WIDE), BF16),
            pltpu.VMEM((2, NCHIP, 4, WIDE), BF16),
            pltpu.VMEM((8, LAT), F32),
            pltpu.VMEM((NX, NZ, NC, 4, 128), BF16),
            pltpu.VMEM((NX, NZ, NC, 4, 128), BF16),
            dma((11,)),
            dma((2, 2)), dma((2, 2)),
            dma((2, 2)), dma((2, 2)),
            dma((2, 2)), dma((2, 2)),
            dma((2, 2)), dma((2, 2)),
            dma((NX + 1,)), dma((NX + 1,)),
        ],
        compiler_params=pltpu.CompilerParams(
            collective_id=0, has_side_effects=True, vmem_limit_bytes=56 * 1024 * 1024),
    )(
        queries, key_absorb, jnp.swapaxes(latent_cache, 1, 2), page_order, lengths,
        kerple_scale.reshape(1, 128), kerple_rate.reshape(1, 128), value_up, output_weight,
    )
    return out.astype(BF16)


def solution(mesh):
    in_specs = (
        P("rep", None, "ctx", None),
        P("ctx", None, None),
        P("rep", "ctx", None),
        P("rep", "ctx"),
        P("rep"),
        P(),
        P(),
        P("ctx", None, None),
        P("ctx", None),
    )
    out_specs = P("rep", None, "ctx")
    return jax.shard_map(
        per_device, mesh=mesh, in_specs=in_specs, out_specs=out_specs, check_vma=False
    )
```

```python
import functools
import math

import jax
import jax.numpy as jnp
from jax import lax
from jax.experimental import pallas as pl
from jax.experimental.pallas import tpu as pltpu
from jax.sharding import PartitionSpec as P

MESH = pl.DeviceIdType.MESH
F32 = jnp.float32
BF16 = jnp.bfloat16

NX, NZ, NC = 4, 8, 2
LAT, ROPE, NOPE, VDIM = 512, 64, 128, 128
WIDE = 640
SLOTS = 4096
PAGE = 128
D = 7168
DOUT = D // (NX * NZ * NC)
ROWS = 256
HALF = ROWS // 2
NCHIP = NX * NZ
SIGMA = (NOPE + ROPE) ** -0.5
KAPPA = SIGMA * math.log2(math.e)
FLOOR = -1.0e30


def steps(slot):
    return slot % NX, (slot // NX + NZ - 1) % NZ


def hops(slot):
    dx, dz = steps(slot)
    return min(dx, NX - dx) + min(dz, NZ - dz)


SELF = NX
AWAY = sorted((t for t in range(NCHIP) if t != SELF), key=lambda t: -hops(t))
FAR_FIRST_Z = (4, 3, 5, 2, 6, 1, 7, 0)
XCOLS = D // NX


def split3(v):
    hi = v.astype(BF16).astype(F32)
    rest = v - hi
    mid = rest.astype(BF16).astype(F32)
    return hi, mid, rest - mid


def pack_stats(c, l):
    lane = lax.broadcasted_iota(jnp.int32, c.shape, c.ndim - 1)
    out = jnp.zeros_like(c)
    for i, part in enumerate(split3(c) + split3(l)):
        out = jnp.where(lane == i, part, out)
    return out


def unpack_stats(st):
    lane = lax.broadcasted_iota(jnp.int32, st.shape, st.ndim - 1)
    c = jnp.sum(jnp.where(lane < 3, st, 0.0), axis=-1, keepdims=True)
    l = jnp.sum(jnp.where((lane >= 3) & (lane < 6), st, 0.0), axis=-1, keepdims=True)
    return c, l


def kernel(
    q_hbm, ka_hbm, kt_hbm, page_hbm, len_hbm, scale_hbm, rate_hbm, vu_hbm, w_hbm,
    out_ref,
    q_s, x_s, ka_s, kt_s, page_s, len_s, scale_s, rate_s, vu_s, w_s,
    qin0, qin1, qf, qall, s_buf, rate_b, scale_b,
    v_s, pair_send, pair_recv, rs_send, rs_recv, lat_s, o_send, o_recv,
    local_sem, ag_ss, ag_rs, relay_ss, relay_rs, pair_ss, pair_rs, rs_ss, rs_rs,
    o_ss, o_rs,
):
    ctx = lax.axis_index("ctx")
    rep = lax.axis_index("rep")
    chip, c = ctx // NC, ctx % NC
    x, z = chip // NZ, chip % NZ
    sibling = (chip * NC + 1 - c, rep)

    def device(dx, dz):
        return ((((x + dx) % NX) * NZ + (z + dz) % NZ) * NC + c, rep)

    def toward(t):
        dx, dz = steps(t)
        return device(dx, dz)

    def back(t):
        dx, dz = steps(t)
        return device(NX - dx, NZ - dz)

    barrier = pltpu.get_barrier_semaphore()
    for t in AWAY:
        pl.semaphore_signal(barrier, inc=1, device_id=toward(t), device_id_type=MESH)
    pl.semaphore_signal(barrier, inc=1, device_id=sibling, device_id_type=MESH)

    loads = {
        name: pltpu.make_async_copy(src, dst, local_sem.at[i])
        for i, (name, src, dst) in enumerate((
            ("q", q_hbm, q_s),
            ("ka", ka_hbm, ka_s),
            ("scale", scale_hbm, scale_s),
            ("rate", rate_hbm, rate_s),
            ("page", page_hbm, page_s),
            ("len", len_hbm, len_s),
            ("k0", kt_hbm.at[0], kt_s.at[0, pl.ds(0, LAT + ROPE)]),
            ("k1", kt_hbm.at[1, pl.ds(0, LAT)], kt_s.at[1, pl.ds(0, LAT)]),
            ("k1r", kt_hbm.at[1, pl.ds(LAT, ROPE)], kt_s.at[1, pl.ds(LAT + ROPE, ROPE)]),
            ("vu", vu_hbm, vu_s),
            ("w", w_hbm, w_s),
        ))
    }
    for name, load in loads.items():
        if name not in ("vu", "w"):
            load.start()

    loads["q"].wait()
    for r in range(2):
        for q in range(2):
            for hh in range(2):
                x_s[pl.ds(4 * r + 2 * hh + q, 1), :] = q_s[r, q, pl.ds(hh, 1), :].astype(F32)
    loads["ka"].wait()
    xq = x_s[...]
    nope = xq[:, :NOPE].astype(BF16)
    lat0 = jnp.dot(nope, ka_s[0], preferred_element_type=F32)
    lat1 = jnp.dot(nope, ka_s[1], preferred_element_type=F32)
    row8 = lax.broadcasted_iota(jnp.int32, (8, LAT), 0)
    lat = jnp.where((row8 // 2) % 2 == 0, lat0, lat1)
    qin0[SELF, :, pl.ds(0, LAT)] = lat[:4].astype(BF16)
    qin0[SELF, :, pl.ds(LAT, ROPE)] = xq[:4, NOPE:].astype(BF16)
    qin0[SELF, :, pl.ds(LAT + ROPE, ROPE)] = xq[4:, NOPE:].astype(BF16)
    qin1[SELF] = lat[4:].astype(BF16)

    kt_s[0, pl.ds(LAT + ROPE, ROPE), :] = jnp.zeros((ROPE, SLOTS), BF16)
    kt_s[1, pl.ds(LAT, ROPE), :] = jnp.zeros((ROPE, SLOTS), BF16)
    o_send[...] = jnp.zeros_like(o_send)
    row = lax.broadcasted_iota(jnp.int32, (ROWS, 128), 0)
    lane = lax.broadcasted_iota(jnp.int32, (ROWS, 128), 1)
    slot = (row // 128) * 16 + (row // 4) % 16
    from_x = (x + NX - slot % NX) % NX
    from_z = (z + 2 * NZ - (slot // NX + NZ - 1)) % NZ
    core = (c + (row // 64) % 2) % NC
    head = ((from_x * NZ + from_z) * NC + core) * 2 + (row // 2) % 2
    hot = lane == head
    loads["scale"].wait()
    loads["rate"].wait()
    rate_col = jnp.sum(jnp.where(hot, rate_s[...], 0.0), axis=-1, keepdims=True)
    scale_col = jnp.sum(jnp.where(hot, scale_s[...], 0.0), axis=-1, keepdims=True)
    rate_b[...] = jnp.broadcast_to(rate_col, (ROWS, 128))
    scale_b[...] = jnp.broadcast_to(scale_col * (1.0 / SIGMA), (ROWS, 128))
    loads["page"].wait()
    loads["len"].wait()

    def transpose(r):
        for i in range(8):
            cols = pl.ds(i * (SLOTS // 8), SLOTS // 8)
            v_s[r, cols, :] = kt_s[r, pl.ds(0, LAT), cols].T

    pl.semaphore_wait(barrier, len(AWAY) + 1)

    qin = (qin0, qin1)

    def ag_copy(r, t):
        return pltpu.make_async_remote_copy(
            src_ref=qin[r].at[SELF], dst_ref=qin[r].at[t],
            send_sem=ag_ss.at[r, t // 16], recv_sem=ag_rs.at[r, t // 16],
            device_id=toward(t), device_id_type=MESH)

    def ag_all(r, b):
        some = qin[r].at[pl.ds(0, 15 if b == 0 else 16)]
        return pltpu.make_async_remote_copy(
            src_ref=some, dst_ref=some, send_sem=ag_ss.at[r, b], recv_sem=ag_rs.at[r, b],
            device_id=sibling, device_id_type=MESH)

    for r, b in ((0, 0), (0, 1), (1, 1), (1, 0)):
        for t in AWAY:
            if t // 16 == b:
                ag_copy(r, t).start()


    loads["k0"].wait()
    transpose(0)
    loads["k1"].wait()
    loads["k1r"].wait()
    loads["vu"].start()
    loads["w"].start()
    transpose(1)

    def relay_copy(r, b):
        return pltpu.make_async_remote_copy(
            src_ref=qall.at[r, b, 0], dst_ref=qall.at[r, b, 1],
            send_sem=relay_ss.at[r, b], recv_sem=relay_rs.at[r, b],
            device_id=sibling, device_id_type=MESH)

    def relay(r, b):
        ag_all(r, b).wait_recv()
        for i in range(16):
            t, rows = 16 * b + i, pl.ds(4 * i, 4)
            if r == 0:
                qf[rows, :] = qin0[t].astype(F32)
            else:
                qf[rows, pl.ds(0, LAT)] = qin1[t].astype(F32)
                qf[rows, pl.ds(LAT, 128)] = qin0[t, :, pl.ds(LAT, 128)].astype(F32)
        qall[r, b, 0] = qf[...].astype(BF16)
        relay_copy(r, b).start()

    sub8 = lax.broadcasted_iota(jnp.int32, (8, 128), 0)
    lane8 = lax.broadcasted_iota(jnp.int32, (8, 128), 1)
    offset = (sub8 % 2 - lane8).astype(F32)

    def scores(r, b):
        relay_copy(r, b).wait_recv()
        rows = pl.ds(HALF * b, HALF)
        rate = rate_b[rows, :].reshape(16, 8, 128)
        scale = scale_b[rows, :].reshape(16, 8, 128)
        base = len_s[r] - 2
        s = jnp.dot(qall[r, b].reshape(HALF, WIDE), kt_s[r], preferred_element_type=F32)
        peak = jnp.full((16, 8, 128), FLOOR, F32)
        for p in range(SLOTS // PAGE):
            dist = (base - page_s[r, p] * PAGE).astype(F32) + offset
            dist = jnp.where(dist >= 0.0, dist, jnp.inf)
            bias = scale * jnp.log(1.0 + rate * dist[None])
            u = s[:, p * PAGE:(p + 1) * PAGE].reshape(16, 8, 128) - bias
            s_buf[r, rows, pl.ds(p * PAGE, PAGE)] = u.reshape(HALF, 128)
            peak = jnp.maximum(peak, u)
        return jnp.max(peak, axis=-1, keepdims=True)

    def sums(r, b, shift):
        total = jnp.zeros((16, 8, 128), F32)
        weights = []
        for p in range(SLOTS // PAGE):
            u = s_buf[r, pl.ds(HALF * b, HALF), pl.ds(p * PAGE, PAGE)].reshape(16, 8, 128)
            w = jnp.exp2(KAPPA * (u - shift))
            total = total + w
            weights.append(w.reshape(HALF, 128).astype(BF16))
        summed = jnp.dot(jnp.concatenate(weights, axis=1), v_s[r], preferred_element_type=F32)
        return jnp.sum(total, axis=-1, keepdims=True), summed

    def pair_copy(r, b):
        return pltpu.make_async_remote_copy(
            src_ref=pair_send.at[r, b], dst_ref=pair_recv.at[r, b],
            send_sem=pair_ss.at[r, b], recv_sem=pair_rs.at[r, b],
            device_id=sibling, device_id_type=MESH)

    def attend(r, b, shift):
        total, summed = sums(r, b, shift)
        shift = jnp.broadcast_to(shift, (16, 8, 128))
        total = jnp.broadcast_to(total, (16, 8, 128))
        pair_send[r, b, :, pl.ds(0, LAT)] = summed[64:].astype(BF16)
        pair_send[r, b, :, pl.ds(LAT, 128)] = pack_stats(shift[8:], total[8:]).reshape(64, 128).astype(BF16)
        pair_copy(r, b).start()
        return shift[:8, :, :1], total[:8, :, :1], summed[:64].reshape(8, 8, LAT)

    def rs_copy(r, t):
        return pltpu.make_async_remote_copy(
            src_ref=rs_send.at[r, t], dst_ref=rs_recv.at[r, t],
            send_sem=rs_ss.at[r, t // 16], recv_sem=rs_rs.at[r, t // 16],
            device_id=back(t), device_id_type=MESH)

    def rs_all(r, b):
        some = pl.ds(0, 15 if b == 0 else 16)
        return pltpu.make_async_remote_copy(
            src_ref=rs_send.at[r, some], dst_ref=rs_recv.at[r, some],
            send_sem=rs_ss.at[r, b], recv_sem=rs_rs.at[r, b],
            device_id=sibling, device_id_type=MESH)

    def send_rows(r, b, own):
        c0, l0, mine = own
        pair_copy(r, b).wait_recv()
        theirs = pair_recv[r, b].astype(F32).reshape(8, 8, WIDE)
        c1, l1 = unpack_stats(theirs[..., LAT:])
        shift = jnp.maximum(c0, c1)
        f0, f1 = jnp.exp2(KAPPA * (c0 - shift)), jnp.exp2(KAPPA * (c1 - shift))
        both = mine * f0 + theirs[..., :LAT] * f1
        stats = pack_stats(
            jnp.broadcast_to(shift, (8, 8, 128)), jnp.broadcast_to(l0 * f0 + l1 * f1, (8, 8, 128)))
        for i in range(8):
            for h in range(2):
                t = 16 * b + 2 * i + h
                rs_send[r, t, :, pl.ds(0, LAT)] = both[i, 4 * h:4 * h + 4].astype(BF16)
                rs_send[r, t, :, pl.ds(LAT, 128)] = stats[i, 4 * h:4 * h + 4].astype(BF16)
        for t in AWAY:
            if t // 16 == b:
                rs_copy(r, t).start()
        if b == 0:
            rs_recv[r, SELF] = rs_send[r, SELF]

    def finish_rows(r):
        rs_all(r, 0).wait_recv()
        rs_all(r, 1).wait_recv()
        parts = rs_recv[r].astype(F32)
        ci, li = unpack_stats(parts[..., LAT:])
        f = jnp.exp2(KAPPA * (ci - jnp.max(ci, axis=0, keepdims=True)))
        total = jnp.sum(parts[..., :LAT] * f, axis=0)
        lat_s[pl.ds(4 * r, 4), :] = total / jnp.sum(li * f, axis=0)

    relay(0, 0)
    near0 = scores(0, 0)
    relay(0, 1)
    near0 = attend(0, 0, near0)
    far0 = scores(0, 1)
    relay(1, 1)
    far0 = attend(0, 1, far0)
    send_rows(0, 0, near0)
    far1 = scores(1, 1)
    send_rows(0, 1, far0)
    relay(1, 0)
    far1 = attend(1, 1, far1)
    near1 = scores(1, 0)
    send_rows(1, 1, far1)
    near1 = attend(1, 0, near1)
    send_rows(1, 0, near1)
    loads["vu"].wait()
    loads["w"].wait()
    finish_rows(0)
    finish_rows(1)

    latent = lat_s[...].astype(BF16)
    up0 = jnp.dot(latent, vu_s[0], preferred_element_type=F32)
    up1 = jnp.dot(latent, vu_s[1], preferred_element_type=F32)
    values = jnp.concatenate([up0, pltpu.roll(up1, 6, 0)], axis=1)
    row8 = lax.broadcasted_iota(jnp.int32, values.shape, 0)
    values = jnp.where(row8 < 2, values, pltpu.roll(values, 6, 0)).astype(BF16)

    def o_copy(g, dz, dc):
        zz, cc = (z + dz) % NZ, (c + dc) % NC
        return pltpu.make_async_remote_copy(
            src_ref=o_send.at[g, zz, cc], dst_ref=o_recv.at[g, dz, dc],
            send_sem=o_ss.at[g], recv_sem=o_rs.at[g],
            device_id=((((x + g) % NX) * NZ + zz) * NC + cc, rep), device_id_type=MESH)

    def o_all(g):
        some = pl.ds(0, 8 if g else 7)
        return pltpu.make_async_remote_copy(
            src_ref=o_send.at[g, some], dst_ref=o_recv.at[g, some],
            send_sem=o_ss.at[g], recv_sem=o_rs.at[g],
            device_id=sibling, device_id_type=MESH)

    def sib_copy():
        return pltpu.make_async_remote_copy(
            src_ref=o_send.at[0, z, 1 - c], dst_ref=o_recv.at[0, 0, 1],
            send_sem=o_ss.at[NX], recv_sem=o_rs.at[NX],
            device_id=sibling, device_id_type=MESH)

    for g in (2, 1, 3, 0):
        cols = pl.ds(pl.multiple_of(((x + g) % NX) * XCOLS, XCOLS), XCOLS)
        share = jnp.dot(values, w_s[:, cols], preferred_element_type=F32)
        for j in range(NZ * NC):
            o_send[g, j // NC, j % NC, :, pl.ds(0, DOUT)] = share[:4, j * DOUT:(j + 1) * DOUT].astype(BF16)
        for dz in FAR_FIRST_Z:
            if g or dz:
                for dc in range(NC):
                    o_copy(g, dz, dc).start()
    sib_copy().start()
    o_recv[0, 0, 0] = o_send[0, z, c]
    for g in (0, 1, 3, 2):
        o_all(g).wait_recv()
    sib_copy().wait_recv()
    final = jnp.sum(o_recv[...].reshape(NCHIP * NC, 4, 128).astype(F32), axis=0)
    for r in range(2):
        for q in range(2):
            at = 2 * r + q
            out_ref[r, pl.ds(q, 1), :] = final[at:at + 1, :DOUT]

    for r in range(2):
        for b in range(2):
            ag_all(r, b).wait_send()
            relay_copy(r, b).wait_send()
            pair_copy(r, b).wait_send()
            rs_all(r, b).wait_send()
    for g in range(NX):
        o_all(g).wait_send()
    sib_copy().wait_send()


def per_device(queries, key_absorb, latent_cache, page_order, lengths, kerple_scale, kerple_rate,
               value_up, output_weight):
    any_spec = pl.BlockSpec(memory_space=pl.ANY)
    dma = pltpu.SemaphoreType.DMA
    out = pl.pallas_call(
        kernel,
        out_shape=jax.ShapeDtypeStruct((2, 2, DOUT), F32),
        in_specs=[any_spec] * 9,
        out_specs=pl.BlockSpec(memory_space=pltpu.VMEM),
        scratch_shapes=[
            pltpu.VMEM((2, 2, 2, NOPE + ROPE), BF16),
            pltpu.VMEM((8, NOPE + ROPE), F32),
            pltpu.VMEM((2, NOPE, LAT), BF16),
            pltpu.VMEM((2, WIDE, SLOTS), BF16),
            pltpu.SMEM((2, SLOTS // PAGE), jnp.int32),
            pltpu.SMEM((2,), jnp.int32),
            pltpu.VMEM((1, 128), F32),
            pltpu.VMEM((1, 128), F32),
            pltpu.VMEM((2, LAT, VDIM), BF16),
            pltpu.VMEM((2 * VDIM, D), BF16),
            pltpu.VMEM((NCHIP, 4, WIDE), BF16),
            pltpu.VMEM((NCHIP, 4, LAT), BF16),
            pltpu.VMEM((64, WIDE), F32),
            pltpu.VMEM((2, 2, 2, 64, WIDE), BF16),
            pltpu.VMEM((2, ROWS, SLOTS), F32),
            pltpu.VMEM((ROWS, 128), F32),
            pltpu.VMEM((ROWS, 128), F32),
            pltpu.VMEM((2, SLOTS, LAT), BF16),
            pltpu.VMEM((2, 2, 64, WIDE), BF16),
            pltpu.VMEM((2, 2, 64, WIDE), BF16),
            pltpu.VMEM((2, NCHIP, 4, WIDE), BF16),
            pltpu.VMEM((2, NCHIP, 4, WIDE), BF16),
            pltpu.VMEM((8, LAT), F32),
            pltpu.VMEM((NX, NZ, NC, 4, 128), BF16),
            pltpu.VMEM((NX, NZ, NC, 4, 128), BF16),
            dma((11,)),
            dma((2, 2)), dma((2, 2)),
            dma((2, 2)), dma((2, 2)),
            dma((2, 2)), dma((2, 2)),
            dma((2, 2)), dma((2, 2)),
            dma((NX + 1,)), dma((NX + 1,)),
        ],
        compiler_params=pltpu.CompilerParams(
            collective_id=0, has_side_effects=True, vmem_limit_bytes=56 * 1024 * 1024),
    )(
        queries, key_absorb, jnp.swapaxes(latent_cache, 1, 2), page_order, lengths,
        kerple_scale.reshape(1, 128), kerple_rate.reshape(1, 128), value_up, output_weight,
    )
    return out.astype(BF16)


def solution(mesh):
    in_specs = (
        P("rep", None, "ctx", None),
        P("ctx", None, None),
        P("rep", "ctx", None),
        P("rep", "ctx"),
        P("rep"),
        P(),
        P(),
        P("ctx", None, None),
        P("ctx", None),
    )
    out_specs = P("rep", None, "ctx")
    return jax.shard_map(
        per_device, mesh=mesh, in_specs=in_specs, out_specs=out_specs, check_vma=False
    )
```
